32 devices in a mesh: member: 2 (over x), tile: 16 (over z, y, core).
Axes of the slice: x: 2, y: 2, z: 4, core: 2. Of those that a mesh axis runs over, the one named last changes fastest.
Arguments:
- parent_state: float32 [5, 8, 384, 768], P(None, None, ('member', 'tile')), parts along dimension 2, may hold values from -6 to 6
- nest_state: float32 [32, 5, 8, 36, 144], P(('member', 'tile')), parts along dimension 0, may hold values from -6 to 6
- metrics: float32 [3, 192, 768], P(None, 'tile'), may hold values from 0.5 to 2
- wave_speed: float32 [8], replicated, may hold values from 0.05 to 0.2
- nest_patch: int32 [16], replicated, may hold values from 0 to 255, as said below
Outputs:
- parent_next: float32 [5, 8, 384, 768], P(None, None, ('member', 'tile')), parts along dimension 2
- nest_next: float32 [32, 5, 8, 36, 144], P(('member', 'tile')), parts along dimension 0
The draws below stay inside these ranges and needn't reach their ends.
There are 2 independent parts, one for each index of `member`. The reference program is written for one: setup_inputs(seed, part) draws one part's arguments, and reference() takes and returns one part's arrays. A program takes and returns all parts, laid end to end along the dimension named above; an argument that names none is the same for every part. Nothing has to cross between parts.
Inputs may be any that keep to these rules, and one draw needn't show every extreme that they name: Every device index d equals nest_patch[b] // 16 for exactly one nest block b.
All inputs are finite; a program needn't handle non-finite values.
Results may differ from the reference program's by a relative error of at most 0.0003.
Values sent between devices are 32-bit elements; how exact they have to be, the bound alone decides.
No kernel may reach another device: no remote copies, remote signals or barrier semaphores. Data moves between devices by JAX's collectives and lax.ppermute only.
A program may use at most 128 MiB of HBM per device.

```python
import math
import jax
import jax.numpy as jnp
from jax import lax

L = 8
CX = 12
CY = 768
PBX = 12
PBY = 48
NSTEP = 4
PPD = 16
NEST_BLOCKS = 16
NX = 192
FX = 36
FY = 144


def draw_nest_patch(key, part):
    key = jax.random.fold_in(key, 11)
    first_key, second_key = jax.random.split(key)
    hosts = jax.random.permutation(first_key, NEST_BLOCKS).astype(jnp.int32)
    local = jax.random.randint(second_key, (NEST_BLOCKS,), 0, PPD, dtype=jnp.int32)
    local = jnp.where(hosts == 0, jnp.int32(0), local)
    local = jnp.where(hosts == NEST_BLOCKS - 1, jnp.int32(PPD - 1), local)
    return (hosts * PPD + local).astype(jnp.int32)


def levels(key, dims, shards, smallest, top_value):
    loudness, own = 1.0, jax.random.fold_in(key, 6)
    for dim, parts in shards:
        draws = jnp.exp(jax.random.uniform(jax.random.fold_in(own, dim), (parts,), jnp.float32, smallest / len(shards), top_value / len(shards)))
        loudness = loudness * jnp.repeat(draws, dims[dim] // parts).reshape([-1 if axis == dim else 1 for axis in range(len(dims))])
    return loudness


def normal_values(rng, dims, scale, most, cuts=(), kind=jnp.bfloat16):
    result = scale * jax.random.normal(rng, dims, jnp.float32)
    if cuts:
        result = result * levels(rng, dims, cuts, -0.22, 0.18)
    return jnp.clip(result, -most, most).astype(kind)


def setup_inputs(seed: int = 0, part: int = 0) -> dict:
    key_of = jax.random.split(jax.random.key(seed), 6)
    part_keys = jax.random.split(jax.random.fold_in(key_of[5], part), 6)
    parent_state = normal_values(part_keys[0], (5, L, NX, CY), 1.0, 6.0, ((2, 16),), jnp.float32)
    nest_state = normal_values(part_keys[1], (NEST_BLOCKS, 5, L, FX, FY), 1.0, 6.0, ((0, 16),), jnp.float32)
    metrics = jnp.clip(jnp.exp(math.log(2.0) - 1.3862944 * jax.random.uniform(key_of[2], (3, NX, CY), jnp.float32) ** levels(key_of[2], (3, NX, CY), ((1, 16),), -0.2, 0.2)), 0.5, 2.0)
    wave_speed = jnp.clip(jnp.exp(jax.random.uniform(key_of[3], (L,), jnp.float32, math.log(0.05), math.log(0.2))), 0.05, 0.2)
    nest_patch = draw_nest_patch(jax.random.fold_in(key_of[5], 71), part)
    return {"parent_state": parent_state, "nest_state": nest_state, "metrics": metrics, "wave_speed": wave_speed, "nest_patch": nest_patch}


DIFFUSION = 0.1


def advance(padded, metrics, speeds):
    centre = padded[..., 1:-1, 1:-1]
    eastern = padded[..., 2:, 1:-1]
    western = padded[..., :-2, 1:-1]
    northern = padded[..., 1:-1, 2:]
    southern = padded[..., 1:-1, :-2]
    spread = eastern + western + northern + southern - 4.0 * centre
    across_x = metrics[0]
    across_y = metrics[1]
    per_area = metrics[2]
    height = centre[0] - speeds * per_area * ((centre[1] - western[1]) + (centre[2] - southern[2])) + DIFFUSION * spread[0]
    zonal_wind = centre[1] - speeds * across_x * (eastern[0] - centre[0]) + DIFFUSION * spread[1]
    merid_wind = centre[2] - speeds * across_y * (northern[0] - centre[0]) + DIFFUSION * spread[2]
    thermal = centre[3] - 0.5 * speeds * (centre[1] * (eastern[3] - western[3]) * across_x + centre[2] * (northern[3] - southern[3]) * across_y) + DIFFUSION * spread[3]
    vertical = centre[4] + speeds * (centre[3] - centre[0]) + DIFFUSION * spread[4]
    return jnp.stack([height, zonal_wind, merid_wind, thermal, vertical])


def nest_padded(state, coarse):
    top_line = jnp.repeat(coarse[..., 0, 1:-1], 3, axis=-1)
    bottom_line = jnp.repeat(coarse[..., -1, 1:-1], 3, axis=-1)
    left_line = jnp.repeat(coarse[..., 1:-1, 0], 3, axis=-1)
    right_line = jnp.repeat(coarse[..., 1:-1, -1], 3, axis=-1)
    corner = jnp.zeros(state.shape[:-2] + (1,), jnp.float32)
    middle = jnp.concatenate([left_line[..., None], state, right_line[..., None]], axis=-1)
    top_row = jnp.concatenate([corner, top_line, corner], axis=-1)[..., None, :]
    bottom_row = jnp.concatenate([corner, bottom_line, corner], axis=-1)[..., None, :]
    return jnp.concatenate([top_row, middle, bottom_row], axis=-2)


def nest_run(state, coarse, coarse_metrics, speeds):
    fine_metrics = jnp.repeat(jnp.repeat(coarse_metrics, 3, axis=-2), 3, axis=-1)

    def one_step(index, current):
        return advance(nest_padded(current, coarse), fine_metrics, speeds)

    return lax.fori_loop(0, 3 * NSTEP, one_step, state)


def coarsen(state):
    shaped = state.reshape(state.shape[:-2] + (state.shape[-2] // 3, 3, state.shape[-1] // 3, 3))
    return jnp.sum(shaped, axis=(-3, -1)) * (1.0 / 9.0)


def reference(parent_state, nest_state, metrics, wave_speed, nest_patch):
    per_level = jnp.moveaxis(parent_state, 1, 0)

    def parent_level(operands):
        field, speed_level = operands
        for step in range(NSTEP):
            field = advance(jnp.pad(field, ((0, 0), (1, 1), (1, 1)), mode="wrap"), metrics, speed_level)
        return field

    advanced = jnp.moveaxis(lax.map(parent_level, (per_level, wave_speed)), 0, 1)
    total_rows = parent_state.shape[2]
    total_cols = parent_state.shape[3]
    patches_y = total_cols // PBY
    speeds = wave_speed[:, None, None]

    def nest_block(operands):
        state, patch = operands
        host = patch // PPD
        local = patch % PPD
        row_first = (host * CX + (local // patches_y) * PBX).astype(jnp.int32)
        col_first = ((local % patches_y) * PBY).astype(jnp.int32)
        row_index = (row_first - 1 + jnp.arange(PBX + 2, dtype=jnp.int32)) % total_rows
        col_index = (col_first - 1 + jnp.arange(PBY + 2, dtype=jnp.int32)) % total_cols
        coarse = jnp.take(jnp.take(parent_state, row_index, axis=2), col_index, axis=3)
        coarse_metrics = lax.dynamic_slice(metrics, (jnp.int32(0), row_first, col_first), (3, PBX, PBY))
        final = nest_run(state, coarse, coarse_metrics, speeds)
        return final, coarsen(final), row_first, col_first

    nest_next, averages, rows_first, cols_first = lax.map(nest_block, (nest_state, nest_patch))

    def insert(index, current):
        return lax.dynamic_update_slice(current, averages[index], (jnp.int32(0), jnp.int32(0), rows_first[index], cols_first[index]))

    parent_next = lax.fori_loop(0, nest_state.shape[0], insert, advanced)
    return parent_next, nest_next
```

```python
import functools

import jax
import jax.numpy as jnp
from jax import lax
from jax.experimental import pallas as pl
from jax.experimental.pallas import tpu as pltpu
from jax.sharding import PartitionSpec as P

PBX = 12
PBY = 48
NSTEP = 4
DIFFUSION = 0.1

FIELDS = 5
LEVELS = 8
FX = 3 * PBX
FY = 3 * PBY
LANES = 128
GROUPS = 16
COLS = FY // GROUPS
ROWS = 5
SLOT = 24
META = 8
F32 = jnp.float32
BF16 = jnp.bfloat16
VMEM = pl.BlockSpec(memory_space=pltpu.VMEM)
SMEM = pl.BlockSpec(memory_space=pltpu.SMEM)
ANY = pl.BlockSpec(memory_space=pl.ANY)


def params():
    return pltpu.CompilerParams(vmem_limit_bytes=40 * 1024 * 1024)


def cost(flops, moved):
    return pl.CostEstimate(flops=flops, bytes_accessed=moved, transcendentals=0)


def iota(shape, dim):
    return lax.broadcasted_iota(jnp.int32, shape, dim)


def chooser(mask):
    return jnp.where(mask, 1.0, 0.0).astype(BF16)


def pick(values, matrix, terms):
    total = None
    for term in range(terms):
        part = values.astype(BF16)
        piece = jnp.dot(part, matrix, preferred_element_type=F32)
        total = piece if total is None else total + piece
        if term + 1 < terms:
            values = values - part.astype(F32)
    return total


def level_speeds(speed_ref, index):
    speeds = jnp.zeros(index.shape, F32)
    for level in range(LEVELS):
        speeds = jnp.where(index == level, speed_ref[level], speeds)
    return speeds


def prepare_kernel(
    per_device, patch_ref, parent_ref, metrics_ref, meta_ref, slots_ref, up_ref, down_ref, lines_ref, cells_ref
):
    count = patch_ref.shape[0]
    columns = parent_ref.shape[3]
    rows = parent_ref.shape[2]
    me = lax.axis_index("tile")

    def note(block, carry):
        meta_ref[META + patch_ref[block] // per_device] = block
        return carry

    lax.fori_loop(0, count, note, 0)
    own = meta_ref[META + me]
    after = meta_ref[META + lax.rem(me + 1, count)]
    before = meta_ref[META + lax.rem(me + count - 1, count)]
    meta_ref[0] = patch_ref[me] // per_device
    meta_ref[1] = lax.rem(patch_ref[own], per_device) * PBY
    last_window = columns - 2 * LANES

    def place(block):
        first = lax.rem(patch_ref[block], per_device) * PBY
        window = jnp.minimum(first // LANES * LANES, last_window)
        return first, pl.multiple_of(window, LANES)

    def window_matrix(offset):
        source = iota((2 * LANES, LANES), 0)
        lane = iota((2 * LANES, LANES), 1)
        wanted = offset + 3 * lax.rem(lane, GROUPS) + lane // GROUPS
        return chooser((source == wanted) & (lane < PBY))

    first, window = place(own)
    for kind in range(3):
        cells_ref[pl.ds(kind * 16, PBX), :] = metrics_ref[kind, :, pl.ds(window, 2 * LANES)]
    mets = pick(cells_ref[...], window_matrix(first - window), 3)
    mets = [mets[kind * 16 : kind * 16 + PBX] for kind in range(3)]
    lane = iota((PBX, LANES), 1)
    packed = jnp.where(
        lane < PBY,
        mets[0],
        jnp.where(lane < 2 * PBY, pltpu.roll(mets[1], PBY, 1), pltpu.roll(mets[2], 2 * PBY, 1)),
    )
    edges = pltpu.roll(mets[2], 48, 1)
    left = lax.rem(first + columns - 1, columns)
    right = lax.rem(first + PBY, columns)
    for side, column in enumerate((left, right)):
        block = pl.multiple_of(column // LANES * LANES, LANES)
        spot = lax.rem(column, LANES)
        for field in range(FIELDS):
            for level in range(LEVELS):
                target = 2 * (field * LEVELS + level) + side
                strip = parent_ref[field, level, :, pl.ds(block, LANES)]
                strip = pltpu.roll(strip, lax.rem(target - spot + LANES, LANES), 1)
                edges = jnp.where(lane == target, strip, edges)
    slots_ref[own, pl.ds(0, PBX), :] = edges
    slots_ref[own, pl.ds(PBX, PBX), :] = packed

    sub8 = iota((LEVELS, LANES), 0)
    chunk8 = iota((LEVELS, LANES), 1) // GROUPS
    for block, row in ((after, rows - 1), (before, 0)):
        first, window = place(block)
        for field in range(FIELDS):
            for level in range(LEVELS):
                lines_ref[pl.ds(field * LEVELS + level, 1), :] = parent_ref[
                    field, level, pl.ds(row, 1), pl.ds(window, 2 * LANES)
                ]
        found = pick(lines_ref[...], window_matrix(first - window), 3)
        for field in range(FIELDS):
            values = found[field * LEVELS : (field + 1) * LEVELS]
            for third in range(3):
                turned = pltpu.roll(values, LANES - GROUPS * third, 1) if third else values
                turned = pltpu.roll(turned, 0, 1, stride=GROUPS, stride_axis=0)
                line = jnp.sum(jnp.where(chunk8 == sub8, turned, 0.0), axis=0, keepdims=True)
                slots_ref[block, pl.ds(field * 3 + third, 1), :] = line

    for field in range(FIELDS):
        for level in range(LEVELS):
            up_ref[field * LEVELS + level] = parent_ref[field, level, pl.ds(rows - NSTEP, NSTEP), :]
            down_ref[field * LEVELS + level] = parent_ref[field, level, pl.ds(0, NSTEP), :]
    for kind in range(3):
        up_ref[FIELDS * LEVELS + kind] = metrics_ref[kind, pl.ds(rows - NSTEP, NSTEP), :]
        down_ref[FIELDS * LEVELS + kind] = metrics_ref[kind, pl.ds(0, NSTEP), :]


def prepare(nest_patch, parent_state, metrics, per_device):
    count = nest_patch.shape[0]
    columns = parent_state.shape[3]
    halo = jax.ShapeDtypeStruct((FIELDS * LEVELS + 3, NSTEP, columns), F32)
    return pl.pallas_call(
        functools.partial(prepare_kernel, per_device),
        out_shape=(
            jax.ShapeDtypeStruct((META + count,), jnp.int32),
            jax.ShapeDtypeStruct((count, SLOT, LANES), F32),
            halo,
            halo,
        ),
        in_specs=[SMEM, VMEM, VMEM],
        out_specs=(SMEM, VMEM, VMEM, VMEM),
        scratch_shapes=[
            pltpu.VMEM((FIELDS * LEVELS, 2 * LANES), F32),
            pltpu.VMEM((48, 2 * LANES), F32),
        ],
        compiler_params=params(),
        cost_estimate=cost(4_000_000, 4_000_000),
        name="prepare",
    )(nest_patch, parent_state, metrics)


def swap_chunks(parts):
    chunk = iota((8, LANES), 1) // GROUPS
    parts = list(parts)
    for bit in (1, 2, 4):
        high = (chunk & bit) != 0
        for low_index in range(8):
            if low_index & bit:
                continue
            high_index = low_index | bit
            low_part, high_part = parts[low_index], parts[high_index]
            parts[low_index] = jnp.where(high, pltpu.roll(high_part, GROUPS * bit, 1), low_part)
            parts[high_index] = jnp.where(
                high, high_part, pltpu.roll(low_part, LANES - GROUPS * bit, 1)
            )
    return parts


def column_order(shape, natural_dim):
    natural = iota(shape, natural_dim)
    packed = iota(shape, 1 - natural_dim)
    return chooser(
        (natural == COLS * lax.rem(packed, GROUPS) + packed // GROUPS) & (packed < FY)
    )


HEIGHT = 40


def nest_in_kernel(nest_ref, out_ref, plain_ref, mixed_ref):
    order = column_order((FY, 2 * LANES), 0)
    for level in range(LEVELS):
        plain_ref[pl.ds(level * HEIGHT + 32, 8), :] = jnp.zeros((8, FY), F32)

    def one_field(field, carry):
        for level in range(LEVELS):
            plain_ref[pl.ds(level * HEIGHT, FX), :] = nest_ref[0, field, level]
        mixed = pick(plain_ref[...], order, 2)
        mixed_ref[0] = mixed[:, :LANES]
        mixed_ref[1] = mixed[:, LANES:]
        for row in range(ROWS):
            parts = [
                mixed_ref[0, pl.ds(level * HEIGHT + row, 8, stride=ROWS), :]
                for level in range(LEVELS)
            ]
            extra = mixed_ref[1, pl.ds(row, 8, stride=ROWS), :]
            for level in range(1, LEVELS):
                extra = extra + pltpu.roll(
                    mixed_ref[1, pl.ds(level * HEIGHT + row, 8, stride=ROWS), :],
                    GROUPS * level,
                    1,
                )
            parts = swap_chunks(parts) + [extra]
            for col in range(COLS):
                out_ref[field, col, row] = parts[col]
        return carry

    lax.fori_loop(0, FIELDS, one_field, 0)


PACKED = (FIELDS, COLS, ROWS, 8, LANES)


def nest_in(nest_state):
    return pl.pallas_call(
        nest_in_kernel,
        out_shape=jax.ShapeDtypeStruct(PACKED, F32),
        in_specs=[VMEM],
        out_specs=VMEM,
        scratch_shapes=[
            pltpu.VMEM((LEVELS * HEIGHT, FY), F32),
            pltpu.VMEM((2, LEVELS * HEIGHT, LANES), F32),
        ],
        compiler_params=params(),
        cost_estimate=cost(8_000_000, 6_000_000),
        name="nest_in",
    )(nest_state)


def nest_out_kernel(packed_ref, out_ref, mixed_ref):
    order = column_order((2 * LANES, FY), 1)
    few = iota((8, LANES), 1) < GROUPS

    def one_field(field, carry):
        for row in range(ROWS):
            parts = swap_chunks([packed_ref[field, col, row] for col in range(8)])
            extra = packed_ref[field, 8, row]
            for level in range(LEVELS):
                where = pl.ds(level * HEIGHT + row, 8, stride=ROWS)
                mixed_ref[0, where, :] = parts[level]
                turned = pltpu.roll(extra, LANES - GROUPS * level, 1) if level else extra
                mixed_ref[1, where, :] = jnp.where(few, turned, 0.0)
        mixed = jnp.concatenate([mixed_ref[0], mixed_ref[1]], axis=1)
        found = pick(mixed, order, 2)
        for level in range(LEVELS):
            out_ref[0, field, level] = found[level * HEIGHT : level * HEIGHT + FX]
        return carry

    lax.fori_loop(0, FIELDS, one_field, 0)


def nest_out(packed):
    return pl.pallas_call(
        nest_out_kernel,
        out_shape=jax.ShapeDtypeStruct((1, FIELDS, LEVELS, FX, FY), F32),
        in_specs=[VMEM],
        out_specs=VMEM,
        scratch_shapes=[pltpu.VMEM((2, LEVELS * HEIGHT, LANES), F32)],
        compiler_params=params(),
        cost_estimate=cost(8_000_000, 6_000_000),
        name="nest_out",
    )(packed)


def substep(centre, east, west, north, south, coef, speeds):
    by_area, by_x, by_y, half_x, half_y = coef
    spread = [
        (1.0 - 4.0 * DIFFUSION) * centre[f]
        + DIFFUSION * ((east[f] + west[f]) + (north[f] + south[f]))
        for f in range(FIELDS)
    ]
    height = spread[0] - by_area * ((centre[1] - west[1]) + (centre[2] - south[2]))
    zonal = spread[1] - by_x * (east[0] - centre[0])
    merid = spread[2] - by_y * (north[0] - centre[0])
    theta = spread[3] - (
        centre[1] * (east[3] - west[3]) * half_x + centre[2] * (north[3] - south[3]) * half_y
    )
    vertical = spread[4] + speeds * (centre[3] - centre[0])
    return height, zonal, merid, theta, vertical


def nest_kernel(
    meta_ref, speed_ref, recv_ref, start_ref, out_ref, mean_ref, a_ref, b_ref, coef_ref, rim_ref, sums_ref
):
    count = recv_ref.shape[0]
    host = meta_ref[0]
    lane = iota((8, LANES), 1)
    chunk = lane // GROUPS
    group = lax.rem(lane, GROUPS)
    sub = iota((8, LANES), 0)
    speeds = level_speeds(speed_ref, chunk)

    fine = iota((ROWS * 8, PBX), 0)
    coarse_row = jnp.minimum((ROWS * lax.rem(fine, 8) + fine // 8) // 3, PBX - 1)
    rows = chooser(coarse_row == iota((ROWS * 8, PBX), 1))
    source = recv_ref[host]
    both = jnp.concatenate([source[:PBX], source[PBX:]], axis=1)
    expanded = None
    for term in range(3):
        part = both.astype(BF16)
        piece = jnp.dot(rows, part, preferred_element_type=F32)
        expanded = piece if expanded is None else expanded + piece
        both = both - part.astype(F32)
    edges = expanded[:, :LANES]
    packed = expanded[:, LANES:]
    for row in range(ROWS):
        for index in range(9):
            if index < 8:
                piece = jnp.where(chunk == index, packed[row * 8 : row * 8 + 8], 0.0)
            else:
                piece = jnp.where(chunk == 5, edges[row * 8 : row * 8 + 8], 0.0)
            for shift in (64, 32, 16):
                piece = piece + pltpu.roll(piece, shift, 1)
            piece = piece * speeds
            kind, third = index // 3, index % 3
            if kind == 2:
                coef_ref[third, row, 0] = piece
            else:
                coef_ref[third, row, 1 + kind] = piece
                coef_ref[third, row, 3 + kind] = 0.5 * piece
    spot = iota((LANES, FIELDS * LANES), 0)
    target = iota((LANES, FIELDS * LANES), 1)
    inside = lax.rem(target, GROUPS)
    pair = 2 * (target // GROUPS)
    spread = chooser(
        ((inside == 0) & (spot == pair)) | ((inside == GROUPS - 1) & (spot == pair + 1))
    )
    rim = pick(edges, spread, 3)
    for row in range(ROWS):
        for field in range(FIELDS):
            rim_ref[field, row] = rim[row * 8 : row * 8 + 8, field * LANES : (field + 1) * LANES]

    top = recv_ref[lax.rem(host + count - 1, count), pl.ds(0, 15), :]
    bottom = recv_ref[lax.rem(host + 1, count), pl.ds(0, 15), :]

    def halo(ref, field):
        for row in range(ROWS):
            ref[field, 0, row] = jnp.where(
                group == 0, rim_ref[field, row], pltpu.roll(ref[field, COLS, row], 1, 1)
            )
            ref[field, COLS + 1, row] = jnp.where(
                group == GROUPS - 1,
                rim_ref[field, row],
                pltpu.roll(ref[field, 1, row], LANES - 1, 1),
            )

    for field in range(FIELDS):
        for col in range(COLS):
            index = field * 3 + col // 3
            for row in range(ROWS):
                value = start_ref[field, col, row]
                if row == 1:
                    value = jnp.where(sub == 7, bottom[index : index + 1], value)
                if row == 4:
                    value = jnp.where(sub == 7, top[index : index + 1], value)
                a_ref[field, col + 1, row] = value
        halo(a_ref, field)

    def one_step(src, dst):
        def thirds(third, carry):
            for inner in range(3):
                col = third * 3 + inner + 1
                centre = [[src[f, col, row] for f in range(FIELDS)] for row in range(ROWS)]
                below = [pltpu.roll(centre[ROWS - 1][f], 1, 0) for f in range(FIELDS)]
                above = [pltpu.roll(centre[0][f], 7, 0) for f in range(FIELDS)]
                for row in range(ROWS):
                    east = centre[row + 1] if row + 1 < ROWS else above
                    west = centre[row - 1] if row else below
                    north = [src[f, col + 1, row] for f in range(FIELDS)]
                    south = [src[f, col - 1, row] for f in range(FIELDS)]
                    coef = [coef_ref[third, row, k] for k in range(5)]
                    new = substep(centre[row], east, west, north, south, coef, speeds)
                    for f in range(FIELDS):
                        value = new[f]
                        if row in (1, 4):
                            value = jnp.where(sub == 7, centre[row][f], value)
                        dst[f, col, row] = value
            return carry

        lax.fori_loop(0, 3, thirds, 0)
        for field in range(FIELDS):
            halo(dst, field)

    def two_steps(index, carry):
        one_step(a_ref, b_ref)
        one_step(b_ref, a_ref)
        return carry

    lax.fori_loop(0, 3 * NSTEP // 2, two_steps, 0)

    for field in range(FIELDS):
        for third in range(3):
            index = field * 3 + third
            for row in range(ROWS):
                values = [a_ref[field, third * 3 + k + 1, row] for k in range(3)]
                for k in range(3):
                    out_ref[field, third * 3 + k, row] = values[k]
                sums_ref[pl.ds(index * HEIGHT + row, 8, stride=ROWS), :] = (
                    values[0] + values[1] + values[2]
                )
            total = sums_ref[pl.ds(index * HEIGHT, PBX, stride=3), :]
            for k in (1, 2):
                total = total + sums_ref[pl.ds(index * HEIGHT + k, PBX, stride=3), :]
            mean_ref[index] = total * (1.0 / 9.0)


def nest_run(meta, wave_speed, recv, start, pieces):
    padded = (FIELDS, COLS + 2, ROWS, 8, LANES)
    return pl.pallas_call(
        nest_kernel,
        out_shape=(
            jax.ShapeDtypeStruct(PACKED, F32),
            jax.ShapeDtypeStruct((pieces, PBX, LANES), F32),
        ),
        in_specs=[SMEM, SMEM, VMEM, VMEM],
        out_specs=(VMEM, VMEM),
        scratch_shapes=[
            pltpu.VMEM(padded, F32),
            pltpu.VMEM(padded, F32),
            pltpu.VMEM((3, ROWS, 5, 8, LANES), F32),
            pltpu.VMEM((FIELDS, ROWS, 8, LANES), F32),
            pltpu.VMEM((15 * HEIGHT, LANES), F32),
        ],
        compiler_params=params(),
        cost_estimate=cost(40_000_000, 3_000_000),
        name="nest_run",
    )(meta, wave_speed, recv, start)


def parent_kernel(speed_ref, parent_ref, low_ref, high_ref, metrics_ref, out_ref, a_ref, b_ref, wide_ref):
    rows = parent_ref.shape[2]
    columns = parent_ref.shape[3]
    parts = columns // LANES
    speeds = level_speeds(speed_ref, iota((LEVELS, columns), 0))
    for field in range(FIELDS):
        for level in range(LEVELS):
            index = field * LEVELS + level
            for part in range(parts):
                span = pl.ds(part * LANES, LANES)
                a_ref[field, part, pl.ds(level, NSTEP, stride=8), :] = low_ref[index, :, span]
                a_ref[field, part, pl.ds(NSTEP * 8 + level, rows, stride=8), :] = parent_ref[
                    field, level, :, span
                ]
                a_ref[field, part, pl.ds((NSTEP + rows) * 8 + level, NSTEP, stride=8), :] = (
                    high_ref[index, :, span]
                )
    for kind in range(3):
        wide_ref[kind, pl.ds(0, NSTEP), :] = low_ref[FIELDS * LEVELS + kind]
        wide_ref[kind, pl.ds(NSTEP, rows), :] = metrics_ref[kind]
        wide_ref[kind, pl.ds(NSTEP + rows, NSTEP), :] = high_ref[FIELDS * LEVELS + kind]

    def one_step(src, dst, first, last):
        def one_row(row, carry):
            def line(field, at):
                span = pl.ds(pl.multiple_of(at * 8, 8), 8)
                return jnp.concatenate([src[field, part, span, :] for part in range(parts)], axis=1)

            centre = [line(f, row) for f in range(FIELDS)]
            east = [line(f, row + 1) for f in range(FIELDS)]
            west = [line(f, row - 1) for f in range(FIELDS)]
            north = [pltpu.roll(centre[f], columns - 1, 1) for f in range(FIELDS)]
            south = [pltpu.roll(centre[f], 1, 1) for f in range(FIELDS)]
            met = [wide_ref[kind, pl.ds(row, 1), :] * speeds for kind in range(3)]
            coef = (met[2], met[0], met[1], 0.5 * met[0], 0.5 * met[1])
            new = substep(centre, east, west, north, south, coef, speeds)
            for f in range(FIELDS):
                for part in range(parts):
                    dst[f, part, pl.ds(pl.multiple_of(row * 8, 8), 8), :] = new[f][
                        :, part * LANES : (part + 1) * LANES
                    ]
            return carry

        lax.fori_loop(first, last, one_row, 0)

    refs = (a_ref, b_ref)
    for step in range(NSTEP):
        one_step(refs[step % 2], refs[(step + 1) % 2], step + 1, rows + 2 * NSTEP - 1 - step)
    final = refs[NSTEP % 2]
    for field in range(FIELDS):
        for level in range(LEVELS):
            for part in range(parts):
                out_ref[field, level, :, pl.ds(part * LANES, LANES)] = final[
                    field, part, pl.ds(NSTEP * 8 + level, rows, stride=8), :
                ]


def parent_run(wave_speed, parent_state, low, high, metrics):
    rows, columns = parent_state.shape[2:]
    wide = (FIELDS, columns // LANES, (rows + 2 * NSTEP) * 8, LANES)
    return pl.pallas_call(
        parent_kernel,
        out_shape=jax.ShapeDtypeStruct(parent_state.shape, F32),
        in_specs=[SMEM, VMEM, VMEM, VMEM, VMEM],
        out_specs=VMEM,
        scratch_shapes=[
            pltpu.VMEM(wide, F32),
            pltpu.VMEM(wide, F32),
            pltpu.VMEM((3, rows + 2 * NSTEP + 4, columns), F32),
        ],
        compiler_params=params(),
        cost_estimate=cost(40_000_000, 8_000_000),
        name="parent_run",
    )(wave_speed, parent_state, low, high, metrics)


def reorder_kernel(meta_ref, in_ref, out_ref):
    def one(index, carry):
        out_ref[index] = in_ref[meta_ref[META + index]]
        return carry

    lax.fori_loop(0, in_ref.shape[0], one, 0)


def reorder(meta, pieces):
    return pl.pallas_call(
        reorder_kernel,
        out_shape=jax.ShapeDtypeStruct(pieces.shape, F32),
        in_specs=[SMEM, VMEM],
        out_specs=VMEM,
        compiler_params=params(),
        cost_estimate=cost(100_000, 200_000),
        name="reorder",
    )(meta, pieces)


def insert_kernel(meta_ref, mean_ref, parent_ref, out_ref, rows_ref, window_ref, sem):
    columns = out_ref.shape[3]
    first = meta_ref[1]
    window = pl.multiple_of(
        jnp.minimum(first // LANES * LANES, columns - 2 * LANES), LANES
    )
    fetch = pltpu.make_async_copy(
        parent_ref.at[:, :, :, pl.ds(window, 2 * LANES)], window_ref, sem
    )
    fetch.start()
    offset = first - window
    lane = iota((PBX, LANES), 1)
    for field in range(FIELDS):
        thirds = [mean_ref[field * 3 + third] for third in range(3)]
        for level in range(LEVELS):
            turned = [
                pltpu.roll(thirds[third], (GROUPS * (third - level)) % LANES, 1)
                if third != level
                else thirds[third]
                for third in range(3)
            ]
            rows_ref[pl.ds((field * LEVELS + level) * 16, PBX), :] = jnp.where(
                lane < GROUPS,
                turned[0],
                jnp.where(lane < 2 * GROUPS, turned[1], jnp.where(lane < PBY, turned[2], 0.0)),
            )
    source = iota((LANES, 2 * LANES), 0)
    target = iota((LANES, 2 * LANES), 1)
    order = chooser(
        (target == offset + 3 * lax.rem(source, GROUPS) + source // GROUPS) & (source < PBY)
    )
    found = pick(rows_ref[...], order, 2)
    wide = iota((PBX, 2 * LANES), 1)
    inside = (wide >= offset) & (wide < offset + PBY)
    fetch.wait()
    for field in range(FIELDS):
        for level in range(LEVELS):
            at = (field * LEVELS + level) * 16
            window_ref[field, level] = jnp.where(
                inside, found[at : at + PBX], window_ref[field, level]
            )
    store = pltpu.make_async_copy(window_ref, out_ref.at[:, :, :, pl.ds(window, 2 * LANES)], sem)
    store.start()
    store.wait()


def insert(meta, means, advanced):
    rows = advanced.shape[2]
    return pl.pallas_call(
        insert_kernel,
        out_shape=jax.ShapeDtypeStruct(advanced.shape, F32),
        in_specs=[SMEM, VMEM, ANY],
        out_specs=ANY,
        scratch_shapes=[
            pltpu.VMEM((FIELDS * LEVELS * 16, LANES), F32),
            pltpu.VMEM((FIELDS, LEVELS, rows, 2 * LANES), F32),
            pltpu.SemaphoreType.DMA,
        ],
        input_output_aliases={2: 0},
        compiler_params=params(),
        cost_estimate=cost(4_000_000, 2_000_000),
        name="insert",
    )(meta, means, advanced)


def body(parent_state, nest_state, metrics, wave_speed, nest_patch):
    count = lax.axis_size("tile")
    rows, columns = parent_state.shape[2:]
    per_device = rows // PBX * (columns // PBY)
    forward = [(i, (i + 1) % count) for i in range(count)]
    backward = [(target, source) for source, target in forward]

    meta, slots, up, down = prepare(nest_patch, parent_state, metrics, per_device)
    recv = lax.all_to_all(slots, "tile", 0, 0, tiled=True)
    low = lax.ppermute(up, "tile", forward)
    high = lax.ppermute(down, "tile", backward)
    start = nest_in(nest_state)
    share = -(-15 * PBX // count)
    direct = share == PBX and count >= 15
    final, means = nest_run(meta, wave_speed, recv, start, count if direct else 15)
    if not direct:
        means = means.reshape(15 * PBX, LANES)
        means = jnp.pad(means, ((0, count * share - 15 * PBX), (0, 0)))
        means = means.reshape(count, share, LANES)
    spread = lax.all_to_all(means, "tile", 0, 0, tiled=True)
    advanced = parent_run(wave_speed, parent_state, low, high, metrics)
    returned = lax.all_to_all(reorder(meta, spread), "tile", 0, 0, tiled=True)
    nest_next = nest_out(final)
    if not direct:
        returned = returned.reshape(count * share, LANES)[: 15 * PBX].reshape(15, PBX, LANES)
    parent_next = insert(meta, returned, advanced)
    return (parent_next, nest_next)


def solution(mesh):
    in_specs = (
        P(None, None, ("member", "tile"), None),
        P(("member", "tile"), None, None, None, None),
        P(None, "tile", None),
        P(),
        P(),
    )
    out_specs = (
        P(None, None, ("member", "tile"), None),
        P(("member", "tile"), None, None, None, None),
    )
    return jax.shard_map(body, mesh=mesh, in_specs=in_specs, out_specs=out_specs, check_vma=False)
```

```python
import functools

import jax
import jax.numpy as jnp
from jax import lax
from jax.experimental import pallas as pl
from jax.experimental.pallas import tpu as pltpu
from jax.sharding import PartitionSpec as P

PBX = 12
PBY = 48
NSTEP = 4
DIFFUSION = 0.1

FIELDS = 5
LEVELS = 8
FX = 3 * PBX
FY = 3 * PBY
LANES = 128
GROUPS = 16
COLS = FY // GROUPS
ROWS = 5
SLOT = 24
META = 8
F32 = jnp.float32
BF16 = jnp.bfloat16
VMEM = pl.BlockSpec(memory_space=pltpu.VMEM)
SMEM = pl.BlockSpec(memory_space=pltpu.SMEM)
HBM = pl.BlockSpec(memory_space=pltpu.HBM)
TOKEN = jax.ShapeDtypeStruct((8, LANES), F32)


def params(mebibytes=24):
    return pltpu.CompilerParams(vmem_limit_bytes=mebibytes * 1024 * 1024)


def cost(flops, moved):
    return pl.CostEstimate(flops=flops, bytes_accessed=moved, transcendentals=0)


def iota(shape, dim):
    return lax.broadcasted_iota(jnp.int32, shape, dim)


def chooser(mask):
    return jnp.where(mask, 1.0, 0.0).astype(BF16)


def pick(values, matrix, terms):
    total = None
    for term in range(terms):
        part = values.astype(BF16)
        piece = jnp.dot(part, matrix, preferred_element_type=F32)
        total = piece if total is None else total + piece
        if term + 1 < terms:
            values = values - part.astype(F32)
    return total


def level_speeds(speed_ref, index):
    speeds = jnp.zeros(index.shape, F32)
    for level in range(LEVELS):
        speeds = jnp.where(index == level, speed_ref[level], speeds)
    return speeds


def prepare_kernel(
    per_device,
    patch_ref,
    parent_ref,
    metrics_ref,
    meta_ref,
    slots_ref,
    up_ref,
    down_ref,
    strips_ref,
    lines_ref,
    cells_ref,
    sides_ref,
    sems,
):
    count = patch_ref.shape[0]
    rows, columns = parent_ref.shape[1], parent_ref.shape[3]
    me = lax.axis_index("tile")
    copies = []

    def fetch(source, target):
        copy = pltpu.make_async_copy(source, target, sems.at[len(copies)])
        copy.start()
        copies.append(copy)

    def note(block, carry):
        meta_ref[META + patch_ref[block] // per_device] = block
        return carry

    lax.fori_loop(0, count, note, 0)
    own = meta_ref[META + me]
    after = meta_ref[META + lax.rem(me + 1, count)]
    before = meta_ref[META + lax.rem(me + count - 1, count)]
    meta_ref[0] = patch_ref[me] // per_device
    meta_ref[1] = lax.rem(patch_ref[own], per_device) * PBY
    last_window = columns - 2 * LANES

    def place(block):
        first = lax.rem(patch_ref[block], per_device) * PBY
        window = jnp.minimum(first // LANES * LANES, last_window)
        return first, pl.multiple_of(window, LANES)

    def window_matrix(offset):
        source = iota((2 * LANES, LANES), 0)
        lane = iota((2 * LANES, LANES), 1)
        wanted = offset + 3 * lax.rem(lane, GROUPS) + lane // GROUPS
        return chooser((source == wanted) & (lane < PBY))

    first, window = place(own)
    left = lax.rem(first + columns - 1, columns)
    right = lax.rem(first + PBY, columns)
    beside = ((after, rows - 1), (before, 0))
    for side, column in enumerate((left, right)):
        block = pl.multiple_of(column // LANES * LANES, LANES)
        fetch(parent_ref.at[:, :, :, pl.ds(block, LANES)], strips_ref.at[side])
    for side, (block, row) in enumerate(beside):
        fetch(parent_ref.at[:, row, :, pl.ds(place(block)[1], 2 * LANES)], lines_ref.at[side])
    for index, (target_ref, start) in enumerate(((up_ref, rows - NSTEP), (down_ref, 0))):
        for field in range(FIELDS):
            fetch(
                parent_ref.at[field, pl.ds(start, NSTEP)],
                target_ref.at[pl.ds(field * NSTEP, NSTEP)],
            )
        for kind in range(3):
            sides_ref[index, kind // 2, pl.ds(kind % 2 * NSTEP, NSTEP), :] = metrics_ref[
                kind, pl.ds(start, NSTEP), :
            ]
        fetch(sides_ref.at[index], target_ref.at[pl.ds(FIELDS * NSTEP, 2)])

    for kind in range(3):
        cells_ref[pl.ds(kind * 16, PBX), :] = metrics_ref[kind, :, pl.ds(window, 2 * LANES)]
    mets = pick(cells_ref[...], window_matrix(first - window), 3)
    mets = [mets[kind * 16 : kind * 16 + 16] for kind in range(3)]
    lane = iota((16, LANES), 1)
    packed = jnp.where(
        lane < PBY,
        mets[0],
        jnp.where(lane < 2 * PBY, pltpu.roll(mets[1], PBY, 1), pltpu.roll(mets[2], 2 * PBY, 1)),
    )
    last = jnp.where((lane >= 32) & (lane < PBY), mets[2], 0.0)
    for shift in (64, 32, 16):
        last = last + pltpu.roll(last, shift, 1)
    last = jnp.where(lane // GROUPS == lax.rem(iota((16, LANES), 0), 8), last, 0.0)
    slots_ref[own, pl.ds(8, PBX), :] = packed[:PBX]
    slots_ref[own, pl.ds(20, 1), :] = jnp.sum(last[:8], axis=0, keepdims=True)
    slots_ref[own, pl.ds(21, 1), :] = jnp.sum(last[8:12], axis=0, keepdims=True)

    lane = iota((LEVELS, LANES), 1)
    edges = jnp.zeros((LEVELS, LANES), F32)
    for side, column in enumerate((left, right)):
        copies[side].wait()
        same = chooser(iota((LANES, LANES), 0) == lax.rem(column, LANES))
        strips = strips_ref[side].reshape(FIELDS * PBX * LEVELS, LANES)
        strips = pick(strips, same, 3)
        for field in range(FIELDS):
            for row in range(PBX):
                at = (field * PBX + row) * LEVELS
                target = row * 10 + field * 2 + side
                edges = jnp.where(lane == target, strips[at : at + LEVELS], edges)
    slots_ref[own, pl.ds(0, 8), :] = edges

    for side, (block, row) in enumerate(beside):
        first, window = place(block)
        copies[2 + side].wait()
        lines = lines_ref[side].reshape(FIELDS * LEVELS, 2 * LANES)
        found = pick(lines, window_matrix(first - window), 3)
        found = [found[field * LEVELS : (field + 1) * LEVELS] for field in range(FIELDS)]
        for pair in range(2):
            slots_ref[block, pl.ds(8 * pair, 8), :] = jnp.where(
                lane < PBY, found[2 * pair], pltpu.roll(found[2 * pair + 1], PBY, 1)
            )
        slots_ref[block, pl.ds(16, 8), :] = found[4]
    for copy in copies[4:]:
        copy.wait()


def prepare(nest_patch, parent_state, metrics, per_device):
    count = nest_patch.shape[0]
    columns = parent_state.shape[3]
    halo = jax.ShapeDtypeStruct((FIELDS * NSTEP + 2, LEVELS, columns), F32)
    return pl.pallas_call(
        functools.partial(prepare_kernel, per_device),
        out_shape=(
            jax.ShapeDtypeStruct((META + count,), jnp.int32),
            jax.ShapeDtypeStruct((count, SLOT, LANES), F32),
            halo,
            halo,
        ),
        in_specs=[SMEM, HBM, VMEM],
        out_specs=(SMEM, VMEM, VMEM, VMEM),
        scratch_shapes=[
            pltpu.VMEM((2, FIELDS, PBX, LEVELS, LANES), F32),
            pltpu.VMEM((2, FIELDS, LEVELS, 2 * LANES), F32),
            pltpu.VMEM((48, 2 * LANES), F32),
            pltpu.VMEM((2, 2, LEVELS, columns), F32),
            pltpu.SemaphoreType.DMA((4 + 2 * FIELDS + 2,)),
        ],
        compiler_params=params(60),
        cost_estimate=cost(4_000_000, 4_000_000),
        name="prepare",
    )(nest_patch, parent_state, metrics)


def swap_chunks(parts):
    chunk = iota((8, LANES), 1) // GROUPS
    parts = list(parts)
    for bit in (1, 2, 4):
        high = (chunk & bit) != 0
        for low_index in range(8):
            if low_index & bit:
                continue
            high_index = low_index | bit
            low_part, high_part = parts[low_index], parts[high_index]
            parts[low_index] = jnp.where(high, pltpu.roll(high_part, GROUPS * bit, 1), low_part)
            parts[high_index] = jnp.where(
                high, high_part, pltpu.roll(low_part, LANES - GROUPS * bit, 1)
            )
    return parts


def column_order(shape, natural_dim):
    natural = iota(shape, natural_dim)
    packed = iota(shape, 1 - natural_dim)
    return chooser(
        (natural == COLS * lax.rem(packed, GROUPS) + packed // GROUPS) & (packed < FY)
    )


def nest_in_kernel(nest_ref, out_ref):
    order = column_order((FY, 2 * LANES), 0)

    def one_field(field, carry):
        plain = nest_ref[0, field].reshape(FX * LEVELS, FY)
        mixed = pick(plain, order, 2)
        for row in range(ROWS):
            parts, extra = [], None
            for group in range(8):
                at = (ROWS * group + row) * LEVELS
                if at >= FX * LEVELS:
                    parts.append(jnp.zeros((LEVELS, LANES), F32))
                    continue
                parts.append(mixed[at : at + LEVELS, :LANES])
                piece = mixed[at : at + LEVELS, LANES:]
                extra = extra + pltpu.roll(piece, GROUPS * group, 1) if group else piece
            parts = swap_chunks(parts) + [extra]
            for col in range(COLS):
                out_ref[field, col, row] = parts[col]
        return carry

    lax.fori_loop(0, FIELDS, one_field, 0)


PACKED = (FIELDS, COLS, ROWS, 8, LANES)


def nest_in(nest_state):
    return pl.pallas_call(
        nest_in_kernel,
        out_shape=jax.ShapeDtypeStruct(PACKED, F32),
        in_specs=[VMEM],
        out_specs=VMEM,
        compiler_params=params(),
        cost_estimate=cost(8_000_000, 6_000_000),
        name="nest_in",
    )(nest_state)


def nest_out_kernel(packed_ref, after_ref, out_ref, token_ref, mixed_ref):
    order = column_order((2 * LANES, FY), 1)
    few = iota((8, LANES), 1) < GROUPS

    def one_field(field, carry):
        for row in range(ROWS):
            parts = swap_chunks([packed_ref[field, col, row] for col in range(8)])
            extra = packed_ref[field, 8, row]
            for group in range(8):
                fine = ROWS * group + row
                if fine >= FX:
                    continue
                turned = pltpu.roll(extra, LANES - GROUPS * group, 1) if group else extra
                mixed_ref[pl.ds(fine * LEVELS, LEVELS), pl.ds(0, LANES)] = parts[group]
                mixed_ref[pl.ds(fine * LEVELS, LEVELS), pl.ds(LANES, LANES)] = jnp.where(
                    few, turned, 0.0
                )
        out_ref[0, field] = pick(mixed_ref[...], order, 2).reshape(FX, LEVELS, FY)
        return carry

    lax.fori_loop(0, FIELDS, one_field, 0)

def nest_out(packed, after):
    return pl.pallas_call(
        nest_out_kernel,
        out_shape=(jax.ShapeDtypeStruct((1, FIELDS, FX, LEVELS, FY), F32), TOKEN),
        in_specs=[VMEM, HBM],
        out_specs=(VMEM, HBM),
        scratch_shapes=[pltpu.VMEM((FX * LEVELS, 2 * LANES), F32)],
        compiler_params=params(),
        cost_estimate=cost(8_000_000, 6_000_000),
        name="nest_out",
    )(packed, after)


def substep(centre, east, west, north, south, coef, speeds):
    by_area, by_x, by_y, half_x, half_y = coef
    spread = [
        (1.0 - 4.0 * DIFFUSION) * centre[f]
        + DIFFUSION * ((east[f] + west[f]) + (north[f] + south[f]))
        for f in range(FIELDS)
    ]
    height = spread[0] - by_area * ((centre[1] - west[1]) + (centre[2] - south[2]))
    zonal = spread[1] - by_x * (east[0] - centre[0])
    merid = spread[2] - by_y * (north[0] - centre[0])
    theta = spread[3] - (
        centre[1] * (east[3] - west[3]) * half_x + centre[2] * (north[3] - south[3]) * half_y
    )
    vertical = spread[4] + speeds * (centre[3] - centre[0])
    return height, zonal, merid, theta, vertical


def nest_kernel(
    meta_ref,
    speed_ref,
    recv_ref,
    start_ref,
    out_ref,
    mean_ref,
    token_ref,
    a_ref,
    b_ref,
    coef_ref,
    rim_ref,
):
    count = recv_ref.shape[0]
    host = meta_ref[0]
    lane = iota((8, LANES), 1)
    chunk = lane // GROUPS
    group = lax.rem(lane, GROUPS)
    sub = iota((8, LANES), 0)
    spare = lane >= LANES - GROUPS
    speeds = level_speeds(speed_ref, sub)

    source = recv_ref[host]
    last = [jnp.where(chunk == sub, source[20 + k : 21 + k], 0.0) for k in range(2)]
    for shift in (64, 32, 16):
        last = [piece + pltpu.roll(piece, shift, 1) for piece in last]
    last = jnp.concatenate(last, axis=0)[:PBX]
    fine = iota((64, PBX), 0)
    coarse_row = jnp.minimum((ROWS * (fine // 8) + lax.rem(fine, 8)) // 3, PBX - 1)
    rows = chooser(coarse_row == iota((64, PBX), 1))
    both = jnp.concatenate([source[8:20], last], axis=1)
    expanded = None
    for term in range(3):
        part = both.astype(BF16)
        piece = jnp.dot(rows, part, preferred_element_type=F32)
        expanded = piece if expanded is None else expanded + piece
        both = both - part.astype(F32)
    kinds = swap_chunks([expanded[8 * k : 8 * k + 8, :LANES] for k in range(8)])
    extra = expanded[:8, LANES:]
    for k in range(1, 8):
        extra = jnp.where(chunk == k, expanded[8 * k : 8 * k + 8, LANES:], extra)
    kinds.append(extra)
    for row in range(ROWS):
        for index in range(9):
            piece = kinds[index][row : row + 1] * speeds
            kind, third = index // 3, index % 3
            if kind == 2:
                coef_ref[third, row, 0] = piece
            else:
                coef_ref[third, row, 1 + kind] = piece
                coef_ref[third, row, 3 + kind] = 0.5 * piece
    edges = source[:8]
    for row in range(ROWS):
        mixed = jnp.zeros((8, LANES), F32)
        for k in range(8):
            coarse = min((ROWS * k + row) // 3, PBX - 1)
            shift = (GROUPS * k - 10 * coarse) % LANES
            turned = pltpu.roll(edges, shift, 1) if shift else edges
            mixed = jnp.where(chunk == k, turned, mixed)
        for field in range(FIELDS):
            lefts = pltpu.roll(mixed, LANES - 2 * field, 1) if field else mixed
            rim_ref[field, row] = jnp.where(
                group == 0, lefts, pltpu.roll(mixed, 14 - 2 * field, 1)
            )

    def line_of(slot, index):
        field, third = index // 3, index % 3
        values = recv_ref[slot, pl.ds(field // 2 * 8, 8), :]
        shift = (LANES - GROUPS - PBY * (field % 2) - GROUPS * third) % LANES
        return pltpu.roll(values, shift, 1) if shift else values

    above_slot = lax.rem(host + count - 1, count)
    below_slot = lax.rem(host + 1, count)

    def put(ref, field, col, row, value):
        ref[field, col, row] = value
        if col == COLS:
            ref[field, 0, row] = jnp.where(group == 0, rim_ref[field, row], pltpu.roll(value, 1, 1))
        if col == 1:
            ref[field, COLS + 1, row] = jnp.where(
                group == GROUPS - 1, rim_ref[field, row], pltpu.roll(value, LANES - 1, 1)
            )
        if row == ROWS - 1:
            ref[field, col, ROWS] = pltpu.roll(value, GROUPS, 1)
        if row == 0:
            ref[field, col, ROWS + 1] = pltpu.roll(value, LANES - GROUPS, 1)

    for field in range(FIELDS):
        for col in range(COLS):
            if col % 3 == 0:
                top = line_of(above_slot, field * 3 + col // 3)
                bottom = line_of(below_slot, field * 3 + col // 3)
            for row in range(ROWS):
                value = start_ref[field, col, row]
                if row == 1:
                    value = jnp.where(spare, bottom, value)
                if row == 4:
                    value = jnp.where(spare, top, value)
                put(a_ref, field, col + 1, row, value)

    def one_step(src, dst):
        for col in range(1, COLS + 1):
            third = (col - 1) // 3
            centre = [[src[f, col, row] for f in range(FIELDS)] for row in range(ROWS)]
            for row in range(ROWS):
                east = (
                    centre[row + 1]
                    if row + 1 < ROWS
                    else [src[f, col, ROWS + 1] for f in range(FIELDS)]
                )
                west = centre[row - 1] if row else [src[f, col, ROWS] for f in range(FIELDS)]
                north = [src[f, col + 1, row] for f in range(FIELDS)]
                south = [src[f, col - 1, row] for f in range(FIELDS)]
                coef = [coef_ref[third, row, k] for k in range(5)]
                new = substep(centre[row], east, west, north, south, coef, speeds)
                for f in range(FIELDS):
                    value = new[f]
                    if row in (1, 4):
                        value = jnp.where(spare, centre[row][f], value)
                    put(dst, f, col, row, value)

    def two_steps(index, carry):
        one_step(a_ref, b_ref)
        one_step(b_ref, a_ref)
        return carry

    lax.fori_loop(0, 3 * NSTEP // 2, two_steps, 0)

    for field in range(FIELDS):
        for third in range(3):
            sums = []
            for row in range(ROWS):
                values = [a_ref[field, third * 3 + k + 1, row] for k in range(3)]
                for k in range(3):
                    out_ref[field, third * 3 + k, row] = values[k]
                sums.append(values[0] + values[1] + values[2])
            later = sums + [pltpu.roll(sums[row], LANES - GROUPS, 1) for row in range(2)]
            totals = [
                (later[row] + later[row + 1] + later[row + 2]) * (1.0 / 9.0) for row in range(ROWS)
            ]
            for half in range(2):
                mean = None
                for coarse in range(8 * half, min(8 * half + 8, PBX)):
                    at, row = 3 * coarse // ROWS, 3 * coarse % ROWS
                    shift = GROUPS * (coarse - 8 * half - at) % LANES
                    piece = pltpu.roll(totals[row], shift, 1) if shift else totals[row]
                    mean = piece if mean is None else jnp.where(chunk == coarse % 8, piece, mean)
                mean_ref[field * 3 + third, pl.ds(8 * half, 8), :] = mean

def nest_run(meta, wave_speed, recv, start, pieces):
    padded = (FIELDS, COLS + 2, ROWS + 2, 8, LANES)
    return pl.pallas_call(
        nest_kernel,
        out_shape=(
            jax.ShapeDtypeStruct(PACKED, F32),
            jax.ShapeDtypeStruct((pieces, 16, LANES), F32),
            TOKEN,
        ),
        in_specs=[SMEM, SMEM, VMEM, VMEM],
        out_specs=(VMEM, VMEM, HBM),
        scratch_shapes=[
            pltpu.VMEM(padded, F32),
            pltpu.VMEM(padded, F32),
            pltpu.VMEM((3, ROWS, 5, 8, LANES), F32),
            pltpu.VMEM((FIELDS, ROWS, 8, LANES), F32),
        ],
        compiler_params=params(),
        cost_estimate=cost(40_000_000, 3_000_000),
        name="nest_run",
    )(meta, wave_speed, recv, start)


def parent_kernel(
    speed_ref,
    parent_ref,
    low_ref,
    high_ref,
    metrics_ref,
    after_ref,
    out_ref,
    token_ref,
    a_ref,
    b_ref,
    wide_ref,
    coef_ref,
):
    rows, columns = parent_ref.shape[1], parent_ref.shape[3]
    parts = columns // LANES
    lane = iota((LEVELS, LANES), 1)
    speeds = level_speeds(speed_ref, iota((LEVELS, LANES), 0))
    for field in range(FIELDS):
        for row in range(NSTEP):
            a_ref[field, row] = low_ref[field * NSTEP + row]
            a_ref[field, NSTEP + rows + row] = high_ref[field * NSTEP + row]
        for row in range(rows):
            a_ref[field, NSTEP + row] = parent_ref[field, row]
    for kind in range(3):
        span = pl.ds(kind % 2 * NSTEP, NSTEP)
        wide_ref[kind, pl.ds(0, NSTEP), :] = low_ref[FIELDS * NSTEP + kind // 2, span, :]
        wide_ref[kind, pl.ds(NSTEP, rows), :] = metrics_ref[kind]
        wide_ref[kind, pl.ds(NSTEP + rows, NSTEP), :] = high_ref[FIELDS * NSTEP + kind // 2, span, :]

    for row in range(1, rows + 2 * NSTEP - 1):
        for kind in range(3):
            for part in range(parts):
                span = pl.ds(part * LANES, LANES)
                coef_ref[kind, row, :, span] = wide_ref[kind, pl.ds(row, 1), span] * speeds

    def one_step(src, dst, first, last, moved):
        def one_row(row):
            def block(field, at, part):
                return src[field, at, :, pl.ds(part % parts * LANES, LANES)]

            for part in range(parts):
                centre = [block(f, row, part) for f in range(FIELDS)]
                east = [block(f, row + 1, part) for f in range(FIELDS)]
                west = [block(f, row - 1, part) for f in range(FIELDS)]
                north = [
                    pltpu.roll(
                        jnp.where(lane == 0, block(f, row, part + 1), centre[f]), LANES - 1, 1
                    )
                    for f in range(FIELDS)
                ]
                south = [
                    pltpu.roll(
                        jnp.where(lane == LANES - 1, block(f, row, part + parts - 1), centre[f]), 1, 1
                    )
                    for f in range(FIELDS)
                ]
                span = pl.ds(part * LANES, LANES)
                by_x, by_y, by_area = [coef_ref[kind, row, :, span] for kind in range(3)]
                coef = (by_area, by_x, by_y, 0.5 * by_x, 0.5 * by_y)
                new = substep(centre, east, west, north, south, coef, speeds)
                for f in range(FIELDS):
                    dst[f, row - moved, :, span] = new[f]

        for row in range(first, last):
            one_row(row)

    refs = (a_ref, b_ref)
    for step in range(NSTEP):
        final = step + 1 == NSTEP
        one_step(
            refs[step % 2],
            out_ref if final else refs[(step + 1) % 2],
            step + 1,
            rows + 2 * NSTEP - 1 - step,
            NSTEP if final else 0,
        )


def parent_run(wave_speed, parent_state, low, high, metrics, after):
    rows, columns = parent_state.shape[1], parent_state.shape[3]
    wide = (FIELDS, rows + 2 * NSTEP, LEVELS, columns)
    return pl.pallas_call(
        parent_kernel,
        out_shape=(jax.ShapeDtypeStruct(parent_state.shape, F32), TOKEN),
        in_specs=[SMEM, VMEM, VMEM, VMEM, VMEM, HBM],
        out_specs=(VMEM, HBM),
        scratch_shapes=[
            pltpu.VMEM(wide, F32),
            pltpu.VMEM(wide, F32),
            pltpu.VMEM((3, rows + 2 * NSTEP + 4, columns), F32),
            pltpu.VMEM((3, rows + 2 * NSTEP, LEVELS, columns), F32),
        ],
        compiler_params=params(),
        cost_estimate=cost(40_000_000, 8_000_000),
        name="parent_run",
    )(wave_speed, parent_state, low, high, metrics, after)


def reorder_kernel(meta_ref, in_ref, after_ref, out_ref, token_ref):
    def one(index, carry):
        out_ref[index] = in_ref[meta_ref[META + index]]
        return carry

    lax.fori_loop(0, in_ref.shape[0], one, 0)


def reorder(meta, pieces, after):
    return pl.pallas_call(
        reorder_kernel,
        out_shape=(jax.ShapeDtypeStruct(pieces.shape, F32), TOKEN),
        in_specs=[SMEM, VMEM, HBM],
        out_specs=(VMEM, HBM),
        compiler_params=params(),
        cost_estimate=cost(100_000, 200_000),
        name="reorder",
    )(meta, pieces, after)


def insert_kernel(meta_ref, mean_ref, parent_ref, after_ref, out_ref, rows_ref, window_ref, sem):
    columns = out_ref.shape[3]
    first = meta_ref[1]
    window = pl.multiple_of(jnp.minimum(first // LANES * LANES, columns - 2 * LANES), LANES)
    fetch = pltpu.make_async_copy(
        parent_ref.at[:, :, :, pl.ds(window, 2 * LANES)], window_ref, sem
    )
    fetch.start()
    offset = first - window
    lane = iota((LEVELS, LANES), 1)
    for field in range(FIELDS):
        for row in range(PBX):
            turned = []
            for third in range(3):
                piece = mean_ref[field * 3 + third, pl.ds(row // 8 * 8, 8), :]
                shift = GROUPS * (third - row % 8) % LANES
                turned.append(pltpu.roll(piece, shift, 1) if shift else piece)
            rows_ref[field * PBX + row] = jnp.where(
                lane < GROUPS,
                turned[0],
                jnp.where(lane < 2 * GROUPS, turned[1], jnp.where(lane < PBY, turned[2], 0.0)),
            )
    source = iota((LANES, 2 * LANES), 0)
    target = iota((LANES, 2 * LANES), 1)
    order = chooser(
        (target == offset + 3 * lax.rem(source, GROUPS) + source // GROUPS) & (source < PBY)
    )
    found = pick(rows_ref[...].reshape(FIELDS * PBX * LEVELS, LANES), order, 2)
    found = found.reshape(FIELDS, PBX, LEVELS, 2 * LANES)
    wide = iota((LEVELS, 2 * LANES), 1)
    inside = (wide >= offset) & (wide < offset + PBY)
    fetch.wait()
    for field in range(FIELDS):
        for row in range(PBX):
            window_ref[field, row] = jnp.where(inside, found[field, row], window_ref[field, row])
    store = pltpu.make_async_copy(window_ref, out_ref.at[:, :, :, pl.ds(window, 2 * LANES)], sem)
    store.start()
    store.wait()


def insert(meta, means, advanced, after):
    return pl.pallas_call(
        insert_kernel,
        out_shape=jax.ShapeDtypeStruct(advanced.shape, F32),
        in_specs=[SMEM, VMEM, HBM, HBM],
        out_specs=HBM,
        scratch_shapes=[
            pltpu.VMEM((FIELDS * PBX, LEVELS, LANES), F32),
            pltpu.VMEM((FIELDS, PBX, LEVELS, 2 * LANES), F32),
            pltpu.SemaphoreType.DMA,
        ],
        input_output_aliases={2: 0},
        compiler_params=params(),
        cost_estimate=cost(4_000_000, 2_000_000),
        name="insert",
    )(meta, means, advanced, after)


def body(parent_state, nest_state, metrics, wave_speed, nest_patch):
    count = lax.axis_size("tile")
    rows, columns = parent_state.shape[2:]
    per_device = rows // PBX * (columns // PBY)
    forward = [(i, (i + 1) % count) for i in range(count)]
    backward = [(target, source) for source, target in forward]
    parent_state = jnp.transpose(parent_state, (0, 2, 1, 3))
    nest_state = jnp.transpose(nest_state, (0, 1, 3, 2, 4))

    meta, slots, up, down = prepare(nest_patch, parent_state, metrics, per_device)
    recv = lax.all_to_all(slots, "tile", 0, 0, tiled=True)
    low = lax.ppermute(up, "tile", forward)
    high = lax.ppermute(down, "tile", backward)
    start = nest_in(nest_state)
    direct = 15 <= count < 30
    share = 16 if direct else -(-15 * 16 // count)
    final, means, nested = nest_run(meta, wave_speed, recv, start, count if direct else 15)
    if not direct:
        means = means.reshape(15 * 16, LANES)
        means = jnp.pad(means, ((0, count * share - 15 * 16), (0, 0)))
        means = means.reshape(count, share, LANES)
    spread = lax.all_to_all(means, "tile", 0, 0, tiled=True)
    advanced, stepped = parent_run(wave_speed, parent_state, low, high, metrics, nested)
    mixed, ordered = reorder(meta, spread, stepped)
    returned = lax.all_to_all(mixed, "tile", 0, 0, tiled=True)
    nest_next, unpacked = nest_out(final, ordered)
    if not direct:
        returned = returned.reshape(count * share, LANES)[: 15 * 16].reshape(15, 16, LANES)
    parent_next = insert(meta, returned, advanced, unpacked)
    return (jnp.transpose(parent_next, (0, 2, 1, 3)), jnp.transpose(nest_next, (0, 1, 3, 2, 4)))


def solution(mesh):
    in_specs = (
        P(None, None, ("member", "tile"), None),
        P(("member", "tile"), None, None, None, None),
        P(None, "tile", None),
        P(),
        P(),
    )
    out_specs = (
        P(None, None, ("member", "tile"), None),
        P(("member", "tile"), None, None, None, None),
    )
    return jax.shard_map(body, mesh=mesh, in_specs=in_specs, out_specs=out_specs, check_vma=False)
```

```python
import functools

import jax
import jax.numpy as jnp
from jax import lax
from jax.experimental import pallas as pl
from jax.experimental.pallas import tpu as pltpu
from jax.sharding import PartitionSpec as P

PBX = 12
PBY = 48
NSTEP = 4
DIFFUSION = 0.1

FIELDS = 5
LEVELS = 8
FX = 3 * PBX
FY = 3 * PBY
LANES = 128
GROUPS = 16
COLS = FY // GROUPS
ROWS = 5
SLOT = 24
META = 8
F32 = jnp.float32
BF16 = jnp.bfloat16
VMEM = pl.BlockSpec(memory_space=pltpu.VMEM)
SMEM = pl.BlockSpec(memory_space=pltpu.SMEM)
HBM = pl.BlockSpec(memory_space=pltpu.HBM)
TOKEN = jax.ShapeDtypeStruct((8, LANES), F32)


def params(mebibytes=24):
    return pltpu.CompilerParams(vmem_limit_bytes=mebibytes * 1024 * 1024)


def cost(flops, moved):
    return pl.CostEstimate(flops=flops, bytes_accessed=moved, transcendentals=0)


def iota(shape, dim):
    return lax.broadcasted_iota(jnp.int32, shape, dim)


def chooser(mask):
    return jnp.where(mask, 1.0, 0.0).astype(BF16)


def pick(values, matrix, terms):
    total = None
    for term in range(terms):
        part = values.astype(BF16)
        piece = jnp.dot(part, matrix, preferred_element_type=F32)
        total = piece if total is None else total + piece
        if term + 1 < terms:
            values = values - part.astype(F32)
    return total


def level_speeds(speed_ref, index):
    speeds = jnp.zeros(index.shape, F32)
    for level in range(LEVELS):
        speeds = jnp.where(index == level, speed_ref[level], speeds)
    return speeds


def prepare_kernel(
    per_device,
    patch_ref,
    parent_ref,
    metrics_ref,
    meta_ref,
    slots_ref,
    near_ref,
    far_ref,
    mine_ref,
    cells_ref,
    sides_ref,
    sems,
):
    count = patch_ref.shape[0]
    rows, columns = parent_ref.shape[1], parent_ref.shape[3]
    me = lax.axis_index("tile")
    copies = []

    def fetch(source, target):
        copy = pltpu.make_async_copy(source, target, sems.at[len(copies)])
        copy.start()
        copies.append(copy)

    def note(block, carry):
        meta_ref[META + patch_ref[block] // per_device] = block
        return carry

    odd = lax.rem(me, 2)
    for index, target_ref in enumerate((near_ref, far_ref)):
        start = (rows - NSTEP) * (1 - odd if index == 0 else odd)
        for field in range(FIELDS):
            fetch(
                parent_ref.at[field, pl.ds(start, NSTEP)],
                target_ref.at[pl.ds(field * NSTEP, NSTEP)],
            )
        for kind in range(3):
            sides_ref[index, kind // 2, pl.ds(kind % 2 * NSTEP, NSTEP), :] = jnp.where(
                odd == index,
                metrics_ref[kind, pl.ds(rows - NSTEP, NSTEP), :],
                metrics_ref[kind, pl.ds(0, NSTEP), :],
            )
        fetch(sides_ref.at[index], target_ref.at[pl.ds(FIELDS * NSTEP, 2)])

    lax.fori_loop(0, count, note, 0)
    own = meta_ref[META + me]
    after = meta_ref[META + lax.rem(me + 1, count)]
    before = meta_ref[META + lax.rem(me + count - 1, count)]
    meta_ref[0] = patch_ref[me] // per_device
    meta_ref[1] = lax.rem(patch_ref[own], per_device) * PBY
    last_window = columns - 2 * LANES

    def place(block):
        first = lax.rem(patch_ref[block], per_device) * PBY
        window = jnp.minimum(first // LANES * LANES, last_window)
        return first, pl.multiple_of(window, LANES)

    def window_matrix(offset):
        source = iota((2 * LANES, LANES), 0)
        lane = iota((2 * LANES, LANES), 1)
        wanted = offset + 3 * lax.rem(lane, GROUPS) + lane // GROUPS
        return chooser((source == wanted) & (lane < PBY))

    first, window = place(own)
    left = lax.rem(first + columns - 1, columns)
    right = lax.rem(first + PBY, columns)
    beside = ((after, rows - 1), (before, 0))
    for kind in range(3):
        cells_ref[pl.ds(kind * 16, PBX), :] = metrics_ref[kind, :, pl.ds(window, 2 * LANES)]
    mets = pick(cells_ref[...], window_matrix(first - window), 3)
    mets = [mets[kind * 16 : kind * 16 + 16] for kind in range(3)]
    lane = iota((16, LANES), 1)
    packed = jnp.where(
        lane < PBY,
        mets[0],
        jnp.where(lane < 2 * PBY, pltpu.roll(mets[1], PBY, 1), pltpu.roll(mets[2], 2 * PBY, 1)),
    )
    last = jnp.where((lane >= 32) & (lane < PBY), mets[2], 0.0)
    for shift in (64, 32, 16):
        last = last + pltpu.roll(last, shift, 1)
    last = jnp.where(lane // GROUPS == lax.rem(iota((16, LANES), 0), 8), last, 0.0)
    mine_ref[0, pl.ds(8, PBX), :] = packed[:PBX]
    mine_ref[0, pl.ds(20, 1), :] = jnp.sum(last[:8], axis=0, keepdims=True)
    mine_ref[0, pl.ds(21, 1), :] = jnp.sum(last[8:12], axis=0, keepdims=True)

    lane = iota((LEVELS, LANES), 1)
    edges = jnp.zeros((LEVELS, LANES), F32)
    for side, column in enumerate((left, right)):
        block = pl.multiple_of(column // LANES * LANES, LANES)
        same = chooser(iota((LANES, LANES), 0) == lax.rem(column, LANES))
        strips = parent_ref[:, :, :, pl.ds(block, LANES)].reshape(FIELDS * PBX * LEVELS, LANES)
        strips = pick(strips, same, 3)
        for field in range(FIELDS):
            for row in range(PBX):
                at = (field * PBX + row) * LEVELS
                target = row * 10 + field * 2 + side
                edges = jnp.where(lane == target, strips[at : at + LEVELS], edges)
    mine_ref[0, pl.ds(0, 8), :] = edges
    fetch(mine_ref.at[0], slots_ref.at[own])

    for side, (block, row) in enumerate(beside):
        first, window = place(block)
        lines = parent_ref[:, row, :, pl.ds(window, 2 * LANES)]
        lines = lines.reshape(FIELDS * LEVELS, 2 * LANES)
        found = pick(lines, window_matrix(first - window), 3)
        found = [found[field * LEVELS : (field + 1) * LEVELS] for field in range(FIELDS)]
        for pair in range(2):
            mine_ref[1 + side, pl.ds(8 * pair, 8), :] = jnp.where(
                lane < PBY, found[2 * pair], pltpu.roll(found[2 * pair + 1], PBY, 1)
            )
        mine_ref[1 + side, pl.ds(16, 8), :] = found[4]
        fetch(mine_ref.at[1 + side], slots_ref.at[block])
    for copy in copies:
        copy.wait()


def prepare(nest_patch, parent_state, metrics, per_device):
    count = nest_patch.shape[0]
    columns = parent_state.shape[3]
    halo = jax.ShapeDtypeStruct((FIELDS * NSTEP + 2, LEVELS, columns), F32)
    return pl.pallas_call(
        functools.partial(prepare_kernel, per_device),
        out_shape=(
            jax.ShapeDtypeStruct((META + count,), jnp.int32),
            jax.ShapeDtypeStruct((count, SLOT, LANES), F32),
            halo,
            halo,
        ),
        in_specs=[SMEM, VMEM, VMEM],
        out_specs=(SMEM, HBM, HBM, HBM),
        scratch_shapes=[
            pltpu.VMEM((3, SLOT, LANES), F32),
            pltpu.VMEM((48, 2 * LANES), F32),
            pltpu.VMEM((2, 2, LEVELS, columns), F32),
            pltpu.SemaphoreType.DMA((3 + 2 * (FIELDS + 1),)),
        ],
        compiler_params=params(60),
        cost_estimate=cost(4_000_000, 4_000_000),
        name="prepare",
    )(nest_patch, parent_state, metrics)


def swap_chunks(parts):
    chunk = iota((8, LANES), 1) // GROUPS
    parts = list(parts)
    for bit in (1, 2, 4):
        high = (chunk & bit) != 0
        for low_index in range(8):
            if low_index & bit:
                continue
            high_index = low_index | bit
            low_part, high_part = parts[low_index], parts[high_index]
            parts[low_index] = jnp.where(high, pltpu.roll(high_part, GROUPS * bit, 1), low_part)
            parts[high_index] = jnp.where(
                high, high_part, pltpu.roll(low_part, LANES - GROUPS * bit, 1)
            )
    return parts


def column_order(shape, natural_dim):
    natural = iota(shape, natural_dim)
    packed = iota(shape, 1 - natural_dim)
    return chooser(
        (natural == COLS * lax.rem(packed, GROUPS) + packed // GROUPS) & (packed < FY)
    )


def nest_in_kernel(nest_ref, out_ref):
    order = column_order((FY, 2 * LANES), 0)

    def one_field(field, carry):
        plain = nest_ref[0, field].reshape(FX * LEVELS, FY)
        mixed = pick(plain, order, 2)
        for row in range(ROWS):
            parts, extra = [], None
            for group in range(8):
                at = (ROWS * group + row) * LEVELS
                if at >= FX * LEVELS:
                    parts.append(jnp.zeros((LEVELS, LANES), F32))
                    continue
                parts.append(mixed[at : at + LEVELS, :LANES])
                piece = mixed[at : at + LEVELS, LANES:]
                extra = extra + pltpu.roll(piece, GROUPS * group, 1) if group else piece
            parts = swap_chunks(parts) + [extra]
            for col in range(COLS):
                out_ref[field, col, row] = parts[col]
        return carry

    lax.fori_loop(0, FIELDS, one_field, 0)


PACKED = (FIELDS, COLS, ROWS, 8, LANES)


def nest_in(nest_state):
    return pl.pallas_call(
        nest_in_kernel,
        out_shape=jax.ShapeDtypeStruct(PACKED, F32),
        in_specs=[VMEM],
        out_specs=VMEM,
        compiler_params=params(),
        cost_estimate=cost(8_000_000, 6_000_000),
        name="nest_in",
    )(nest_state)


def nest_out_kernel(packed_ref, after_ref, out_ref, token_ref, mixed_ref):
    order = column_order((2 * LANES, FY), 1)
    few = iota((8, LANES), 1) < GROUPS

    def one_field(field, carry):
        for row in range(ROWS):
            parts = swap_chunks([packed_ref[field, col, row] for col in range(8)])
            extra = packed_ref[field, 8, row]
            for group in range(8):
                fine = ROWS * group + row
                if fine >= FX:
                    continue
                turned = pltpu.roll(extra, LANES - GROUPS * group, 1) if group else extra
                mixed_ref[pl.ds(fine * LEVELS, LEVELS), pl.ds(0, LANES)] = parts[group]
                mixed_ref[pl.ds(fine * LEVELS, LEVELS), pl.ds(LANES, LANES)] = jnp.where(
                    few, turned, 0.0
                )
        out_ref[0, field] = pick(mixed_ref[...], order, 2).reshape(FX, LEVELS, FY)
        return carry

    lax.fori_loop(0, FIELDS, one_field, 0)

def nest_out(packed, after):
    return pl.pallas_call(
        nest_out_kernel,
        out_shape=(jax.ShapeDtypeStruct((1, FIELDS, FX, LEVELS, FY), F32), TOKEN),
        in_specs=[VMEM, HBM],
        out_specs=(VMEM, HBM),
        scratch_shapes=[pltpu.VMEM((FX * LEVELS, 2 * LANES), F32)],
        compiler_params=params(),
        cost_estimate=cost(8_000_000, 6_000_000),
        name="nest_out",
    )(packed, after)


def substep(centre, east, west, north, south, coef, speeds):
    by_area, by_x, by_y, half_x, half_y = coef
    spread = [
        (1.0 - 4.0 * DIFFUSION) * centre[f]
        + DIFFUSION * ((east[f] + west[f]) + (north[f] + south[f]))
        for f in range(FIELDS)
    ]
    height = spread[0] - by_area * ((centre[1] - west[1]) + (centre[2] - south[2]))
    zonal = spread[1] - by_x * (east[0] - centre[0])
    merid = spread[2] - by_y * (north[0] - centre[0])
    theta = spread[3] - (
        centre[1] * (east[3] - west[3]) * half_x + centre[2] * (north[3] - south[3]) * half_y
    )
    vertical = spread[4] + speeds * (centre[3] - centre[0])
    return height, zonal, merid, theta, vertical


def nest_kernel(
    meta_ref,
    speed_ref,
    recv_ref,
    start_ref,
    out_ref,
    mean_ref,
    token_ref,
    a_ref,
    b_ref,
    coef_ref,
    rim_ref,
):
    count = recv_ref.shape[0]
    host = meta_ref[0]
    lane = iota((8, LANES), 1)
    chunk = lane // GROUPS
    group = lax.rem(lane, GROUPS)
    sub = iota((8, LANES), 0)
    spare = lane >= LANES - GROUPS
    speeds = level_speeds(speed_ref, sub)

    source = recv_ref[host]
    last = [jnp.where(chunk == sub, source[20 + k : 21 + k], 0.0) for k in range(2)]
    for shift in (64, 32, 16):
        last = [piece + pltpu.roll(piece, shift, 1) for piece in last]
    last = jnp.concatenate(last, axis=0)[:PBX]
    fine = iota((64, PBX), 0)
    coarse_row = jnp.minimum((ROWS * (fine // 8) + lax.rem(fine, 8)) // 3, PBX - 1)
    rows = chooser(coarse_row == iota((64, PBX), 1))
    both = jnp.concatenate([source[8:20], last], axis=1)
    expanded = None
    for term in range(3):
        part = both.astype(BF16)
        piece = jnp.dot(rows, part, preferred_element_type=F32)
        expanded = piece if expanded is None else expanded + piece
        both = both - part.astype(F32)
    kinds = swap_chunks([expanded[8 * k : 8 * k + 8, :LANES] for k in range(8)])
    extra = expanded[:8, LANES:]
    for k in range(1, 8):
        extra = jnp.where(chunk == k, expanded[8 * k : 8 * k + 8, LANES:], extra)
    kinds.append(extra)
    for row in range(ROWS):
        for index in range(9):
            piece = kinds[index][row : row + 1] * speeds
            kind, third = index // 3, index % 3
            if kind == 2:
                coef_ref[third, row, 0] = piece
            else:
                coef_ref[third, row, 1 + kind] = piece
                coef_ref[third, row, 3 + kind] = 0.5 * piece
    edges = source[:8]
    for row in range(ROWS):
        mixed = jnp.zeros((8, LANES), F32)
        for k in range(8):
            coarse = min((ROWS * k + row) // 3, PBX - 1)
            shift = (GROUPS * k - 10 * coarse) % LANES
            turned = pltpu.roll(edges, shift, 1) if shift else edges
            mixed = jnp.where(chunk == k, turned, mixed)
        for field in range(FIELDS):
            lefts = pltpu.roll(mixed, LANES - 2 * field, 1) if field else mixed
            rim_ref[field, row] = jnp.where(
                group == 0, lefts, pltpu.roll(mixed, 14 - 2 * field, 1)
            )

    def line_of(slot, index):
        field, third = index // 3, index % 3
        values = recv_ref[slot, pl.ds(field // 2 * 8, 8), :]
        shift = (LANES - GROUPS - PBY * (field % 2) - GROUPS * third) % LANES
        return pltpu.roll(values, shift, 1) if shift else values

    above_slot = lax.rem(host + count - 1, count)
    below_slot = lax.rem(host + 1, count)

    def put(ref, field, col, row, value):
        ref[field, col, row] = value
        if col == COLS:
            ref[field, 0, row] = jnp.where(
                group == 0, rim_ref[field, row], pltpu.roll(value, 1, 1)
            )
        if col == 1:
            ref[field, COLS + 1, row] = jnp.where(
                group == GROUPS - 1, rim_ref[field, row], pltpu.roll(value, LANES - 1, 1)
            )
        if row == ROWS - 1:
            ref[field, col, ROWS] = pltpu.roll(value, GROUPS, 1)
        if row == 0:
            ref[field, col, ROWS + 1] = pltpu.roll(value, LANES - GROUPS, 1)

    for field in range(FIELDS):
        for col in range(COLS):
            if col % 3 == 0:
                top = line_of(above_slot, field * 3 + col // 3)
                bottom = line_of(below_slot, field * 3 + col // 3)
            for row in range(ROWS):
                value = start_ref[field, col, row]
                if row == 1:
                    value = jnp.where(spare, bottom, value)
                if row == 4:
                    value = jnp.where(spare, top, value)
                put(a_ref, field, col + 1, row, value)

    def one_step(src, dst):
        def at(field, col, row):
            return src[field, col, row]

        for col in range(1, COLS + 1):
            third = (col - 1) // 3
            centre = [[at(f, col, row) for f in range(FIELDS)] for row in range(ROWS)]
            for row in range(ROWS):
                below = row + 1 if row + 1 < ROWS else ROWS + 1
                east = centre[below] if below < ROWS else [at(f, col, below) for f in range(FIELDS)]
                west = centre[row - 1] if row else [at(f, col, ROWS) for f in range(FIELDS)]
                north = [at(f, col + 1, row) for f in range(FIELDS)]
                south = [at(f, col - 1, row) for f in range(FIELDS)]
                coef = [coef_ref[third, row, k] for k in range(5)]
                new = substep(centre[row], east, west, north, south, coef, speeds)
                for f in range(FIELDS):
                    value = new[f]
                    if row in (1, 4):
                        value = jnp.where(spare, centre[row][f], value)
                    put(dst, f, col, row, value)

    def two_steps(index, carry):
        one_step(a_ref, b_ref)
        one_step(b_ref, a_ref)
        return carry

    lax.fori_loop(0, 3 * NSTEP // 2, two_steps, 0)

    for field in range(FIELDS):
        for third in range(3):
            sums = []
            for row in range(ROWS):
                values = [a_ref[field, third * 3 + k + 1, row] for k in range(3)]
                for k in range(3):
                    out_ref[field, third * 3 + k, row] = values[k]
                sums.append(values[0] + values[1] + values[2])
            later = sums + [pltpu.roll(sums[row], LANES - GROUPS, 1) for row in range(2)]
            totals = [
                (later[row] + later[row + 1] + later[row + 2]) * (1.0 / 9.0) for row in range(ROWS)
            ]
            for half in range(2):
                mean = None
                for coarse in range(8 * half, min(8 * half + 8, PBX)):
                    at, row = 3 * coarse // ROWS, 3 * coarse % ROWS
                    shift = GROUPS * (coarse - 8 * half - at) % LANES
                    piece = pltpu.roll(totals[row], shift, 1) if shift else totals[row]
                    mean = piece if mean is None else jnp.where(chunk == coarse % 8, piece, mean)
                mean_ref[field * 3 + third, pl.ds(8 * half, 8), :] = mean

def nest_run(meta, wave_speed, recv, start, pieces):
    padded = (FIELDS, COLS + 2, ROWS + 2, 8, LANES)
    return pl.pallas_call(
        nest_kernel,
        out_shape=(
            jax.ShapeDtypeStruct(PACKED, F32),
            jax.ShapeDtypeStruct((pieces, 16, LANES), F32),
            TOKEN,
        ),
        in_specs=[SMEM, SMEM, VMEM, VMEM],
        out_specs=(VMEM, VMEM, HBM),
        scratch_shapes=[
            pltpu.VMEM(padded, F32),
            pltpu.VMEM(padded, F32),
            pltpu.VMEM((3, ROWS, 5, 8, LANES), F32),
            pltpu.VMEM((FIELDS, ROWS, 8, LANES), F32),
        ],
        compiler_params=params(24),
        cost_estimate=cost(40_000_000, 3_000_000),
        name="nest_run",
    )(meta, wave_speed, recv, start)


def patch_window(meta_ref, columns):
    first = meta_ref[1]
    return first, pl.multiple_of(jnp.minimum(first // LANES * LANES, columns - 2 * LANES), LANES)


def parent_kernel(
    meta_ref,
    speed_ref,
    parent_ref,
    near_ref,
    far_ref,
    metrics_ref,
    after_ref,
    out_ref,
    window_ref,
    a_ref,
    b_ref,
    last_ref,
    sides_ref,
    coef_ref,
    sems,
):
    rows, columns = parent_ref.shape[1], parent_ref.shape[3]
    parts = columns // LANES
    odd = lax.rem(lax.axis_index("tile"), 2)
    copies = []

    def move(source, target):
        copies.append(pltpu.make_async_copy(source, target, sems.at[len(copies)]))
        copies[-1].start()

    move(parent_ref, a_ref.at[:, pl.ds(NSTEP, rows)])
    for index, source_ref in enumerate((near_ref, far_ref)):
        high = 1 - odd if index == 0 else odd
        for field in range(FIELDS):
            move(
                source_ref.at[pl.ds(field * NSTEP, NSTEP)],
                a_ref.at[field, pl.ds((NSTEP + rows) * high, NSTEP)],
            )
        move(source_ref.at[pl.ds(FIELDS * NSTEP, 2)], sides_ref.at[high])

    lane = iota((LEVELS, LANES), 1)
    speeds = level_speeds(speed_ref, iota((LEVELS, LANES), 0))

    def put_coef(row):
        for kind in range(3):
            if NSTEP <= row < NSTEP + rows:
                line = metrics_ref[kind, pl.ds(row - NSTEP, 1), :]
            else:
                inner = row if row < NSTEP else row - NSTEP - rows
                line = sides_ref[
                    int(row >= NSTEP), kind // 2, pl.ds(kind % 2 * NSTEP + inner, 1), :
                ]
            for part in range(parts):
                span = slice(part * LANES, (part + 1) * LANES)
                coef_ref[kind, row, :, span] = line[:, span] * speeds

    def one_step(src, dst, lines, moved):
        def one_row(row):
            def block(field, at, part):
                return src[field, at, :, pl.ds(part % parts * LANES, LANES)]

            for part in range(parts):
                centre = [block(f, row, part) for f in range(FIELDS)]
                east = [block(f, row + 1, part) for f in range(FIELDS)]
                west = [block(f, row - 1, part) for f in range(FIELDS)]
                north = [
                    pltpu.roll(
                        jnp.where(lane == 0, block(f, row, part + 1), centre[f]), LANES - 1, 1
                    )
                    for f in range(FIELDS)
                ]
                south = [
                    pltpu.roll(
                        jnp.where(lane == LANES - 1, block(f, row, part + parts - 1), centre[f]), 1, 1
                    )
                    for f in range(FIELDS)
                ]
                span = pl.ds(part * LANES, LANES)
                by_x, by_y, by_area = [coef_ref[kind, row, :, span] for kind in range(3)]
                coef = (by_area, by_x, by_y, 0.5 * by_x, 0.5 * by_y)
                new = substep(centre, east, west, north, south, coef, speeds)
                for f in range(FIELDS):
                    dst[f, row - moved, :, span] = new[f]

        for row in lines:
            one_row(row)

    for row in range(NSTEP, NSTEP + rows):
        put_coef(row)
    copies[0].wait()
    inner = range(NSTEP + 1, NSTEP + rows - 1)
    one_step(a_ref, b_ref, inner, 0)
    for copy in copies[1:]:
        copy.wait()
    outer = [row for row in range(1, rows + 2 * NSTEP - 1) if row not in inner]
    for row in outer:
        if not NSTEP <= row < NSTEP + rows:
            put_coef(row)
    one_step(a_ref, b_ref, outer, 0)
    for step in range(1, NSTEP - 1):
        source, target = (a_ref, b_ref) if step % 2 == 0 else (b_ref, a_ref)
        one_step(source, target, range(step + 1, rows + 2 * NSTEP - 1 - step), 0)
    window = patch_window(meta_ref, columns)[1]
    done = len(copies)
    for row in range(rows):
        one_step(a_ref if NSTEP % 2 else b_ref, last_ref, [NSTEP + row], NSTEP)
        move(last_ref.at[:, row], out_ref.at[:, row])
        move(last_ref.at[:, row, :, pl.ds(window, 2 * LANES)], window_ref.at[:, row])
    for copy in copies[done:]:
        copy.wait()


def parent_run(meta, wave_speed, parent_state, near, far, metrics, after):
    rows, columns = parent_state.shape[1], parent_state.shape[3]
    wide = (FIELDS, rows + 2 * NSTEP, LEVELS, columns)
    return pl.pallas_call(
        parent_kernel,
        out_shape=(
            jax.ShapeDtypeStruct(parent_state.shape, F32),
            jax.ShapeDtypeStruct((FIELDS, rows, LEVELS, 2 * LANES), F32),
        ),
        in_specs=[SMEM, SMEM, HBM, HBM, HBM, VMEM, HBM],
        out_specs=(HBM, HBM),
        scratch_shapes=[
            pltpu.VMEM(wide, F32),
            pltpu.VMEM(wide, F32),
            pltpu.VMEM(parent_state.shape, F32),
            pltpu.VMEM((2, 2, LEVELS, columns), F32),
            pltpu.VMEM((3, rows + 2 * NSTEP, LEVELS, columns), F32),
            pltpu.SemaphoreType.DMA((1 + 2 * (FIELDS + 1) + 2 * rows,)),
        ],
        compiler_params=params(),
        cost_estimate=cost(40_000_000, 8_000_000),
        name="parent_run",
    )(meta, wave_speed, parent_state, near, far, metrics, after)


def reorder_kernel(meta_ref, in_ref, after_ref, out_ref, token_ref, sem):
    def copy(index):
        return pltpu.make_async_copy(in_ref.at[meta_ref[META + index]], out_ref.at[index], sem)

    def start(index, carry):
        copy(index).start()
        return carry

    lax.fori_loop(0, in_ref.shape[0], start, 0)
    pltpu.make_async_copy(in_ref, out_ref, sem).wait()


def reorder(meta, pieces, after):
    return pl.pallas_call(
        reorder_kernel,
        out_shape=(jax.ShapeDtypeStruct(pieces.shape, F32), TOKEN),
        in_specs=[SMEM, VMEM, HBM],
        out_specs=(HBM, HBM),
        scratch_shapes=[pltpu.SemaphoreType.DMA],
        compiler_params=params(),
        cost_estimate=cost(100_000, 200_000),
        name="reorder",
    )(meta, pieces, after)


def insert_kernel(meta_ref, mean_ref, old_ref, parent_ref, out_ref, rows_ref, window_ref, sems):
    first, window = patch_window(meta_ref, out_ref.shape[3])
    offset = first - window
    lane = iota((LEVELS, LANES), 1)
    for field in range(FIELDS):
        for row in range(PBX):
            turned = []
            for third in range(3):
                piece = mean_ref[field * 3 + third, pl.ds(row // 8 * 8, 8), :]
                shift = GROUPS * (third - row % 8) % LANES
                turned.append(pltpu.roll(piece, shift, 1) if shift else piece)
            rows_ref[field * PBX + row] = jnp.where(
                lane < GROUPS,
                turned[0],
                jnp.where(lane < 2 * GROUPS, turned[1], jnp.where(lane < PBY, turned[2], 0.0)),
            )
    source = iota((LANES, 2 * LANES), 0)
    target = iota((LANES, 2 * LANES), 1)
    order = chooser(
        (target == offset + 3 * lax.rem(source, GROUPS) + source // GROUPS) & (source < PBY)
    )
    found = pick(rows_ref[...].reshape(FIELDS * PBX * LEVELS, LANES), order, 2)
    found = found.reshape(FIELDS, PBX, LEVELS, 2 * LANES)
    wide = iota((LEVELS, 2 * LANES), 1)
    inside = (wide >= offset) & (wide < offset + PBY)
    copies = []
    for field in range(FIELDS):
        for row in range(PBX):
            window_ref[field, row] = jnp.where(inside, found[field, row], old_ref[field, row])
        copies.append(
            pltpu.make_async_copy(
                window_ref.at[field],
                out_ref.at[field, :, :, pl.ds(window, 2 * LANES)],
                sems.at[field],
            )
        )
        copies[-1].start()
    for copy in copies:
        copy.wait()


def insert(meta, means, window, advanced):
    return pl.pallas_call(
        insert_kernel,
        out_shape=jax.ShapeDtypeStruct(advanced.shape, F32),
        in_specs=[SMEM, VMEM, VMEM, HBM],
        out_specs=HBM,
        scratch_shapes=[
            pltpu.VMEM((FIELDS * PBX, LEVELS, LANES), F32),
            pltpu.VMEM((FIELDS, PBX, LEVELS, 2 * LANES), F32),
            pltpu.SemaphoreType.DMA((FIELDS,)),
        ],
        input_output_aliases={3: 0},
        compiler_params=params(),
        cost_estimate=cost(4_000_000, 2_000_000),
        name="insert",
    )(meta, means, window, advanced)


def body(parent_state, nest_state, metrics, wave_speed, nest_patch):
    count = lax.axis_size("tile")
    rows, columns = parent_state.shape[2:]
    per_device = rows // PBX * (columns // PBY)
    near_pairs = [(i, i ^ 1) for i in range(count)]
    far_pairs = [(i, (i - 1 + 2 * (i % 2)) % count) for i in range(count)]
    parent_state = jnp.transpose(parent_state, (0, 2, 1, 3))
    nest_state = jnp.transpose(nest_state, (0, 1, 3, 2, 4))

    meta, slots, near, far = prepare(nest_patch, parent_state, metrics, per_device)
    recv = lax.all_to_all(slots, "tile", 0, 0, tiled=True)
    start = nest_in(nest_state)
    recv, near, far, start = lax.optimization_barrier((recv, near, far, start))
    near = lax.ppermute(near, "tile", near_pairs)
    far = lax.ppermute(far, "tile", far_pairs)
    direct = 15 <= count < 30
    share = 16 if direct else -(-15 * 16 // count)
    final, means, nested = nest_run(meta, wave_speed, recv, start, count if direct else 15)
    if not direct:
        means = means.reshape(15 * 16, LANES)
        means = jnp.pad(means, ((0, count * share - 15 * 16), (0, 0)))
        means = means.reshape(count, share, LANES)
    spread = lax.all_to_all(means, "tile", 0, 0, tiled=True)
    nest_next, unpacked = nest_out(final, nested)
    mixed, ordered = reorder(meta, spread, unpacked)
    returned = lax.all_to_all(mixed, "tile", 0, 0, tiled=True)
    advanced, window = parent_run(meta, wave_speed, parent_state, near, far, metrics, ordered)
    if not direct:
        returned = returned.reshape(count * share, LANES)[: 15 * 16].reshape(15, 16, LANES)
    parent_next = insert(meta, returned, window, advanced)
    return (jnp.transpose(parent_next, (0, 2, 1, 3)), jnp.transpose(nest_next, (0, 1, 3, 2, 4)))


def solution(mesh):
    in_specs = (
        P(None, None, ("member", "tile"), None),
        P(("member", "tile"), None, None, None, None),
        P(None, "tile", None),
        P(),
        P(),
    )
    out_specs = (
        P(None, None, ("member", "tile"), None),
        P(("member", "tile"), None, None, None, None),
    )
    return jax.shard_map(body, mesh=mesh, in_specs=in_specs, out_specs=out_specs, check_vma=False)
```

```python
import functools

import jax
import jax.numpy as jnp
from jax import lax
from jax.experimental import pallas as pl
from jax.experimental.pallas import tpu as pltpu
from jax.sharding import PartitionSpec as P

PBX = 12
PBY = 48
NSTEP = 4
DIFFUSION = 0.1

FIELDS = 5
LEVELS = 8
FX = 3 * PBX
FY = 3 * PBY
LANES = 128
GROUPS = 16
COLS = FY // GROUPS
ROWS = 5
SLOT = 24
META = 8
F32 = jnp.float32
BF16 = jnp.bfloat16
VMEM = pl.BlockSpec(memory_space=pltpu.VMEM)
SMEM = pl.BlockSpec(memory_space=pltpu.SMEM)
HBM = pl.BlockSpec(memory_space=pltpu.HBM)
TOKEN = jax.ShapeDtypeStruct((8, LANES), F32)


def params(mebibytes=24):
    return pltpu.CompilerParams(vmem_limit_bytes=mebibytes * 1024 * 1024)


def cost(flops, moved):
    return pl.CostEstimate(flops=flops, bytes_accessed=moved, transcendentals=0)


def iota(shape, dim):
    return lax.broadcasted_iota(jnp.int32, shape, dim)


def chooser(mask):
    return jnp.where(mask, 1.0, 0.0).astype(BF16)


def pick(values, matrix, terms):
    total = None
    for term in range(terms):
        part = values.astype(BF16)
        piece = jnp.dot(part, matrix, preferred_element_type=F32)
        total = piece if total is None else total + piece
        if term + 1 < terms:
            values = values - part.astype(F32)
    return total


def level_speeds(speed_ref, index):
    speeds = jnp.zeros(index.shape, F32)
    for level in range(LEVELS):
        speeds = jnp.where(index == level, speed_ref[level], speeds)
    return speeds


def prepare_kernel(
    per_device,
    patch_ref,
    parent_ref,
    metrics_ref,
    meta_ref,
    slots_ref,
    near_ref,
    far_ref,
    mine_ref,
    cells_ref,
    sides_ref,
    sems,
):
    count = patch_ref.shape[0]
    rows, columns = parent_ref.shape[1], parent_ref.shape[3]
    me = lax.axis_index("tile")
    copies = []

    def fetch(source, target):
        copy = pltpu.make_async_copy(source, target, sems.at[len(copies)])
        copy.start()
        copies.append(copy)

    def note(block, carry):
        meta_ref[META + patch_ref[block] // per_device] = block
        return carry

    odd = lax.rem(me, 2)
    for index, target_ref in enumerate((near_ref, far_ref)):
        start = (rows - NSTEP) * (1 - odd if index == 0 else odd)
        for field in range(FIELDS):
            fetch(
                parent_ref.at[field, pl.ds(start, NSTEP)],
                target_ref.at[pl.ds(field * NSTEP, NSTEP)],
            )
        for kind in range(3):
            sides_ref[index, kind // 2, pl.ds(kind % 2 * NSTEP, NSTEP), :] = jnp.where(
                odd == index,
                metrics_ref[kind, pl.ds(rows - NSTEP, NSTEP), :],
                metrics_ref[kind, pl.ds(0, NSTEP), :],
            )
        fetch(sides_ref.at[index], target_ref.at[pl.ds(FIELDS * NSTEP, 2)])

    lax.fori_loop(0, count, note, 0)
    own = meta_ref[META + me]
    after = meta_ref[META + lax.rem(me + 1, count)]
    before = meta_ref[META + lax.rem(me + count - 1, count)]
    meta_ref[0] = patch_ref[me] // per_device
    meta_ref[1] = lax.rem(patch_ref[own], per_device) * PBY
    last_window = columns - 2 * LANES

    def place(block):
        first = lax.rem(patch_ref[block], per_device) * PBY
        window = jnp.minimum(first // LANES * LANES, last_window)
        return first, pl.multiple_of(window, LANES)

    def window_matrix(offset):
        source = iota((2 * LANES, LANES), 0)
        lane = iota((2 * LANES, LANES), 1)
        wanted = offset + 3 * lax.rem(lane, GROUPS) + lane // GROUPS
        return chooser((source == wanted) & (lane < PBY))

    first, window = place(own)
    left = lax.rem(first + columns - 1, columns)
    right = lax.rem(first + PBY, columns)
    beside = ((after, rows - 1), (before, 0))
    for kind in range(3):
        cells_ref[pl.ds(kind * 16, PBX), :] = metrics_ref[kind, :, pl.ds(window, 2 * LANES)]
    mets = pick(cells_ref[...], window_matrix(first - window), 2)
    mets = [mets[kind * 16 : kind * 16 + 16] for kind in range(3)]
    lane = iota((16, LANES), 1)
    packed = jnp.where(
        lane < PBY,
        mets[0],
        jnp.where(lane < 2 * PBY, pltpu.roll(mets[1], PBY, 1), pltpu.roll(mets[2], 2 * PBY, 1)),
    )
    last = jnp.where((lane >= 32) & (lane < PBY), mets[2], 0.0)
    for shift in (64, 32, 16):
        last = last + pltpu.roll(last, shift, 1)
    last = jnp.where(lane // GROUPS == lax.rem(iota((16, LANES), 0), 8), last, 0.0)
    mine_ref[0, pl.ds(8, PBX), :] = packed[:PBX]
    mine_ref[0, pl.ds(20, 1), :] = jnp.sum(last[:8], axis=0, keepdims=True)
    mine_ref[0, pl.ds(21, 1), :] = jnp.sum(last[8:12], axis=0, keepdims=True)

    lane = iota((LEVELS, LANES), 1)
    edges = jnp.zeros((LEVELS, LANES), F32)
    for side, column in enumerate((left, right)):
        block = pl.multiple_of(column // LANES * LANES, LANES)
        same = chooser(iota((LANES, LANES), 0) == lax.rem(column, LANES))
        strips = parent_ref[:, :, :, pl.ds(block, LANES)].reshape(FIELDS * PBX * LEVELS, LANES)
        strips = pick(strips, same, 2)
        for field in range(FIELDS):
            for row in range(PBX):
                at = (field * PBX + row) * LEVELS
                target = row * 10 + field * 2 + side
                edges = jnp.where(lane == target, strips[at : at + LEVELS], edges)
    mine_ref[0, pl.ds(0, 8), :] = edges
    fetch(mine_ref.at[0], slots_ref.at[own])

    for side, (block, row) in enumerate(beside):
        first, window = place(block)
        lines = parent_ref[:, row, :, pl.ds(window, 2 * LANES)]
        lines = lines.reshape(FIELDS * LEVELS, 2 * LANES)
        found = pick(lines, window_matrix(first - window), 2)
        found = [found[field * LEVELS : (field + 1) * LEVELS] for field in range(FIELDS)]
        for pair in range(2):
            mine_ref[1 + side, pl.ds(8 * pair, 8), :] = jnp.where(
                lane < PBY, found[2 * pair], pltpu.roll(found[2 * pair + 1], PBY, 1)
            )
        mine_ref[1 + side, pl.ds(16, 8), :] = found[4]
        fetch(mine_ref.at[1 + side], slots_ref.at[block])
    for copy in copies:
        copy.wait()


def prepare(nest_patch, parent_state, metrics, per_device):
    count = nest_patch.shape[0]
    columns = parent_state.shape[3]
    halo = jax.ShapeDtypeStruct((FIELDS * NSTEP + 2, LEVELS, columns), F32)
    return pl.pallas_call(
        functools.partial(prepare_kernel, per_device),
        out_shape=(
            jax.ShapeDtypeStruct((META + count,), jnp.int32),
            jax.ShapeDtypeStruct((count, SLOT, LANES), F32),
            halo,
            halo,
        ),
        in_specs=[SMEM, VMEM, VMEM],
        out_specs=(SMEM, HBM, HBM, HBM),
        scratch_shapes=[
            pltpu.VMEM((3, SLOT, LANES), F32),
            pltpu.VMEM((48, 2 * LANES), F32),
            pltpu.VMEM((2, 2, LEVELS, columns), F32),
            pltpu.SemaphoreType.DMA((3 + 2 * (FIELDS + 1),)),
        ],
        compiler_params=params(60),
        cost_estimate=cost(4_000_000, 4_000_000),
        name="prepare",
    )(nest_patch, parent_state, metrics)


def swap_chunks(parts):
    chunk = iota((8, LANES), 1) // GROUPS
    parts = list(parts)
    for bit in (1, 2, 4):
        high = (chunk & bit) != 0
        for low_index in range(8):
            if low_index & bit:
                continue
            high_index = low_index | bit
            low_part, high_part = parts[low_index], parts[high_index]
            parts[low_index] = jnp.where(high, pltpu.roll(high_part, GROUPS * bit, 1), low_part)
            parts[high_index] = jnp.where(
                high, high_part, pltpu.roll(low_part, LANES - GROUPS * bit, 1)
            )
    return parts


def column_order(shape, natural_dim):
    natural = iota(shape, natural_dim)
    packed = iota(shape, 1 - natural_dim)
    return chooser(
        (natural == COLS * lax.rem(packed, GROUPS) + packed // GROUPS) & (packed < FY)
    )


def nest_in_kernel(nest_ref, out_ref):
    order = column_order((FY, 2 * LANES), 0)

    def one_field(field, carry):
        plain = nest_ref[0, field].reshape(FX * LEVELS, FY)
        mixed = pick(plain, order, 2)
        for row in range(ROWS):
            parts, extra = [], None
            for group in range(8):
                at = (ROWS * group + row) * LEVELS
                if at >= FX * LEVELS:
                    parts.append(jnp.zeros((LEVELS, LANES), F32))
                    continue
                parts.append(mixed[at : at + LEVELS, :LANES])
                piece = mixed[at : at + LEVELS, LANES:]
                extra = extra + pltpu.roll(piece, GROUPS * group, 1) if group else piece
            parts = swap_chunks(parts) + [extra]
            for col in range(COLS):
                out_ref[field, col, row] = parts[col]
        return carry

    lax.fori_loop(0, FIELDS, one_field, 0)


PACKED = (FIELDS, COLS, ROWS, 8, LANES)


def nest_in(nest_state):
    return pl.pallas_call(
        nest_in_kernel,
        out_shape=jax.ShapeDtypeStruct(PACKED, F32),
        in_specs=[VMEM],
        out_specs=VMEM,
        compiler_params=params(),
        cost_estimate=cost(8_000_000, 6_000_000),
        name="nest_in",
    )(nest_state)


def nest_out_kernel(packed_ref, after_ref, out_ref, token_ref, mixed_ref):
    order = column_order((2 * LANES, FY), 1)
    few = iota((8, LANES), 1) < GROUPS

    def one_field(field, carry):
        for row in range(ROWS):
            parts = swap_chunks([packed_ref[field, col, row] for col in range(8)])
            extra = packed_ref[field, 8, row]
            for group in range(8):
                fine = ROWS * group + row
                if fine >= FX:
                    continue
                turned = pltpu.roll(extra, LANES - GROUPS * group, 1) if group else extra
                mixed_ref[pl.ds(fine * LEVELS, LEVELS), pl.ds(0, LANES)] = parts[group]
                mixed_ref[pl.ds(fine * LEVELS, LEVELS), pl.ds(LANES, LANES)] = jnp.where(
                    few, turned, 0.0
                )
        out_ref[0, field] = pick(mixed_ref[...], order, 2).reshape(FX, LEVELS, FY)
        return carry

    lax.fori_loop(0, FIELDS, one_field, 0)

def nest_out(packed, after):
    return pl.pallas_call(
        nest_out_kernel,
        out_shape=(jax.ShapeDtypeStruct((1, FIELDS, FX, LEVELS, FY), F32), TOKEN),
        in_specs=[VMEM, HBM],
        out_specs=(VMEM, HBM),
        scratch_shapes=[pltpu.VMEM((FX * LEVELS, 2 * LANES), F32)],
        compiler_params=params(),
        cost_estimate=cost(8_000_000, 6_000_000),
        name="nest_out",
    )(packed, after)


def substep(centre, east, west, north, south, coef, speeds):
    by_area, by_x, by_y, half_x, half_y = coef
    spread = [
        (1.0 - 4.0 * DIFFUSION) * centre[f]
        + DIFFUSION * ((east[f] + west[f]) + (north[f] + south[f]))
        for f in range(FIELDS)
    ]
    height = spread[0] - by_area * ((centre[1] - west[1]) + (centre[2] - south[2]))
    zonal = spread[1] - by_x * (east[0] - centre[0])
    merid = spread[2] - by_y * (north[0] - centre[0])
    theta = spread[3] - (
        centre[1] * (east[3] - west[3]) * half_x + centre[2] * (north[3] - south[3]) * half_y
    )
    vertical = spread[4] + speeds * (centre[3] - centre[0])
    return height, zonal, merid, theta, vertical


def nest_kernel(
    meta_ref,
    speed_ref,
    recv_ref,
    start_ref,
    out_ref,
    mean_ref,
    token_ref,
    a_ref,
    b_ref,
    coef_ref,
    rim_ref,
):
    count = recv_ref.shape[0]
    host = meta_ref[0]
    lane = iota((8, LANES), 1)
    chunk = lane // GROUPS
    group = lax.rem(lane, GROUPS)
    sub = iota((8, LANES), 0)
    spare = lane >= LANES - GROUPS
    speeds = level_speeds(speed_ref, sub)

    source = recv_ref[host]
    last = [jnp.where(chunk == sub, source[20 + k : 21 + k], 0.0) for k in range(2)]
    for shift in (64, 32, 16):
        last = [piece + pltpu.roll(piece, shift, 1) for piece in last]
    last = jnp.concatenate(last, axis=0)[:PBX]
    fine = iota((64, PBX), 0)
    coarse_row = jnp.minimum((ROWS * (fine // 8) + lax.rem(fine, 8)) // 3, PBX - 1)
    rows = chooser(coarse_row == iota((64, PBX), 1))
    both = jnp.concatenate([source[8:20], last], axis=1)
    expanded = None
    for term in range(2):
        part = both.astype(BF16)
        piece = jnp.dot(rows, part, preferred_element_type=F32)
        expanded = piece if expanded is None else expanded + piece
        both = both - part.astype(F32)
    kinds = swap_chunks([expanded[8 * k : 8 * k + 8, :LANES] for k in range(8)])
    extra = expanded[:8, LANES:]
    for k in range(1, 8):
        extra = jnp.where(chunk == k, expanded[8 * k : 8 * k + 8, LANES:], extra)
    kinds.append(extra)
    for row in range(ROWS):
        for index in range(9):
            piece = kinds[index][row : row + 1] * speeds
            kind, third = index // 3, index % 3
            if kind == 2:
                coef_ref[third, row, 0] = piece
            else:
                coef_ref[third, row, 1 + kind] = piece
                coef_ref[third, row, 3 + kind] = 0.5 * piece
    edges = source[:8]
    for row in range(ROWS):
        mixed = jnp.zeros((8, LANES), F32)
        for k in range(8):
            coarse = min((ROWS * k + row) // 3, PBX - 1)
            shift = (GROUPS * k - 10 * coarse) % LANES
            turned = pltpu.roll(edges, shift, 1) if shift else edges
            mixed = jnp.where(chunk == k, turned, mixed)
        for field in range(FIELDS):
            lefts = pltpu.roll(mixed, LANES - 2 * field, 1) if field else mixed
            rim_ref[field, row] = jnp.where(
                group == 0, lefts, pltpu.roll(mixed, 14 - 2 * field, 1)
            )

    def line_of(slot, index):
        field, third = index // 3, index % 3
        values = recv_ref[slot, pl.ds(field // 2 * 8, 8), :]
        shift = (LANES - GROUPS - PBY * (field % 2) - GROUPS * third) % LANES
        return pltpu.roll(values, shift, 1) if shift else values

    above_slot = lax.rem(host + count - 1, count)
    below_slot = lax.rem(host + 1, count)

    def put(ref, field, col, row, value):
        ref[field, col, row] = value
        if col == COLS:
            ref[field, 0, row] = jnp.where(
                group == 0, rim_ref[field, row], pltpu.roll(value, 1, 1)
            )
        if col == 1:
            ref[field, COLS + 1, row] = jnp.where(
                group == GROUPS - 1, rim_ref[field, row], pltpu.roll(value, LANES - 1, 1)
            )
        if row == ROWS - 1:
            ref[field, col, ROWS] = pltpu.roll(value, GROUPS, 1)
        if row == 0:
            ref[field, col, ROWS + 1] = pltpu.roll(value, LANES - GROUPS, 1)

    for field in range(FIELDS):
        for col in range(COLS):
            if col % 3 == 0:
                top = line_of(above_slot, field * 3 + col // 3)
                bottom = line_of(below_slot, field * 3 + col // 3)
            for row in range(ROWS):
                value = start_ref[field, col, row]
                if row == 1:
                    value = jnp.where(spare, bottom, value)
                if row == 4:
                    value = jnp.where(spare, top, value)
                put(a_ref, field, col + 1, row, value)

    def one_step(src, dst):
        def at(field, col, row):
            return src[field, col, row]

        for col in range(1, COLS + 1):
            third = (col - 1) // 3
            centre = [[at(f, col, row) for f in range(FIELDS)] for row in range(ROWS)]
            for row in range(ROWS):
                below = row + 1 if row + 1 < ROWS else ROWS + 1
                east = centre[below] if below < ROWS else [at(f, col, below) for f in range(FIELDS)]
                west = centre[row - 1] if row else [at(f, col, ROWS) for f in range(FIELDS)]
                north = [at(f, col + 1, row) for f in range(FIELDS)]
                south = [at(f, col - 1, row) for f in range(FIELDS)]
                coef = [coef_ref[third, row, k] for k in range(5)]
                new = substep(centre[row], east, west, north, south, coef, speeds)
                for f in range(FIELDS):
                    value = new[f]
                    if row in (1, 4):
                        value = jnp.where(spare, centre[row][f], value)
                    put(dst, f, col, row, value)

    def two_steps(index, carry):
        one_step(a_ref, b_ref)
        one_step(b_ref, a_ref)
        return carry

    lax.fori_loop(0, 3 * NSTEP // 2, two_steps, 0)

    for field in range(FIELDS):
        for third in range(3):
            sums = []
            for row in range(ROWS):
                values = [a_ref[field, third * 3 + k + 1, row] for k in range(3)]
                for k in range(3):
                    out_ref[field, third * 3 + k, row] = values[k]
                sums.append(values[0] + values[1] + values[2])
            later = sums + [pltpu.roll(sums[row], LANES - GROUPS, 1) for row in range(2)]
            totals = [
                (later[row] + later[row + 1] + later[row + 2]) * (1.0 / 9.0) for row in range(ROWS)
            ]
            for half in range(2):
                mean = None
                for coarse in range(8 * half, min(8 * half + 8, PBX)):
                    at, row = 3 * coarse // ROWS, 3 * coarse % ROWS
                    shift = GROUPS * (coarse - 8 * half - at) % LANES
                    piece = pltpu.roll(totals[row], shift, 1) if shift else totals[row]
                    mean = piece if mean is None else jnp.where(chunk == coarse % 8, piece, mean)
                at = 3 * (field * 3 + third)
                if half == 0:
                    mean_ref[at] = mean[:4]
                    mean_ref[at + 1] = mean[4:]
                else:
                    mean_ref[at + 2] = jnp.where(
                        lane[:4] < LANES // 2, mean[:4], pltpu.roll(mean, LANES // 2, 1)[4:]
                    )

def nest_run(meta, wave_speed, recv, start, pieces):
    padded = (FIELDS, COLS + 2, ROWS + 2, 8, LANES)
    return pl.pallas_call(
        nest_kernel,
        out_shape=(
            jax.ShapeDtypeStruct(PACKED, F32),
            jax.ShapeDtypeStruct((pieces * 3, 4, LANES), F32),
            TOKEN,
        ),
        in_specs=[SMEM, SMEM, VMEM, VMEM],
        out_specs=(VMEM, VMEM, HBM),
        scratch_shapes=[
            pltpu.VMEM(padded, F32),
            pltpu.VMEM(padded, F32),
            pltpu.VMEM((3, ROWS, 5, 8, LANES), F32),
            pltpu.VMEM((FIELDS, ROWS, 8, LANES), F32),
        ],
        compiler_params=params(24),
        cost_estimate=cost(40_000_000, 3_000_000),
        name="nest_run",
    )(meta, wave_speed, recv, start)


def patch_window(meta_ref, columns):
    first = meta_ref[1]
    return first, pl.multiple_of(jnp.minimum(first // LANES * LANES, columns - 2 * LANES), LANES)


def parent_kernel(
    meta_ref,
    speed_ref,
    parent_ref,
    near_ref,
    far_ref,
    metrics_ref,
    after_ref,
    out_ref,
    window_ref,
    a_ref,
    b_ref,
    last_ref,
    sides_ref,
    coef_ref,
    sems,
):
    rows, columns = parent_ref.shape[1], parent_ref.shape[3]
    parts = columns // LANES
    odd = lax.rem(lax.axis_index("tile"), 2)
    copies = []

    def move(source, target):
        copies.append(pltpu.make_async_copy(source, target, sems.at[len(copies)]))
        copies[-1].start()

    move(parent_ref, a_ref.at[:, pl.ds(NSTEP, rows)])
    for index, source_ref in enumerate((near_ref, far_ref)):
        high = 1 - odd if index == 0 else odd
        for field in range(FIELDS):
            move(
                source_ref.at[pl.ds(field * NSTEP, NSTEP)],
                a_ref.at[field, pl.ds((NSTEP + rows) * high, NSTEP)],
            )
        move(source_ref.at[pl.ds(FIELDS * NSTEP, 2)], sides_ref.at[high])

    lane = iota((LEVELS, LANES), 1)
    speeds = level_speeds(speed_ref, iota((LEVELS, LANES), 0))

    def put_coef(row):
        for kind in range(3):
            if NSTEP <= row < NSTEP + rows:
                line = metrics_ref[kind, pl.ds(row - NSTEP, 1), :]
            else:
                inner = row if row < NSTEP else row - NSTEP - rows
                line = sides_ref[
                    int(row >= NSTEP), kind // 2, pl.ds(kind % 2 * NSTEP + inner, 1), :
                ]
            for part in range(parts):
                span = slice(part * LANES, (part + 1) * LANES)
                coef_ref[kind, row, :, span] = line[:, span] * speeds

    def one_step(src, dst, lines, moved):
        def one_row(row):
            def block(field, at, part):
                return src[field, at, :, pl.ds(part % parts * LANES, LANES)]

            for part in range(parts):
                centre = [block(f, row, part) for f in range(FIELDS)]
                east = [block(f, row + 1, part) for f in range(FIELDS)]
                west = [block(f, row - 1, part) for f in range(FIELDS)]
                north = [
                    pltpu.roll(
                        jnp.where(lane == 0, block(f, row, part + 1), centre[f]), LANES - 1, 1
                    )
                    for f in range(FIELDS)
                ]
                south = [
                    pltpu.roll(
                        jnp.where(lane == LANES - 1, block(f, row, part + parts - 1), centre[f]), 1, 1
                    )
                    for f in range(FIELDS)
                ]
                span = pl.ds(part * LANES, LANES)
                by_x, by_y, by_area = [coef_ref[kind, row, :, span] for kind in range(3)]
                coef = (by_area, by_x, by_y, 0.5 * by_x, 0.5 * by_y)
                new = substep(centre, east, west, north, south, coef, speeds)
                for f in range(FIELDS):
                    dst[f, row - moved, :, span] = new[f]

        for row in lines:
            one_row(row)

    for row in range(NSTEP, NSTEP + rows):
        put_coef(row)
    copies[0].wait()
    inner = range(NSTEP + 1, NSTEP + rows - 1)
    one_step(a_ref, b_ref, inner, 0)
    for copy in copies[1:]:
        copy.wait()
    outer = [row for row in range(1, rows + 2 * NSTEP - 1) if row not in inner]
    for row in outer:
        if not NSTEP <= row < NSTEP + rows:
            put_coef(row)
    one_step(a_ref, b_ref, outer, 0)
    for step in range(1, NSTEP - 1):
        source, target = (a_ref, b_ref) if step % 2 == 0 else (b_ref, a_ref)
        one_step(source, target, range(step + 1, rows + 2 * NSTEP - 1 - step), 0)
    window = patch_window(meta_ref, columns)[1]
    done = len(copies)
    for row in range(rows):
        one_step(a_ref if NSTEP % 2 else b_ref, last_ref, [NSTEP + row], NSTEP)
        move(last_ref.at[:, row], out_ref.at[:, row])
        move(last_ref.at[:, row, :, pl.ds(window, 2 * LANES)], window_ref.at[:, row])
    for copy in copies[done:]:
        copy.wait()


def parent_run(meta, wave_speed, parent_state, near, far, metrics, after):
    rows, columns = parent_state.shape[1], parent_state.shape[3]
    wide = (FIELDS, rows + 2 * NSTEP, LEVELS, columns)
    return pl.pallas_call(
        parent_kernel,
        out_shape=(
            jax.ShapeDtypeStruct(parent_state.shape, F32),
            jax.ShapeDtypeStruct((FIELDS, rows, LEVELS, 2 * LANES), F32),
        ),
        in_specs=[SMEM, SMEM, HBM, HBM, HBM, VMEM, HBM],
        out_specs=(HBM, HBM),
        scratch_shapes=[
            pltpu.VMEM(wide, F32),
            pltpu.VMEM(wide, F32),
            pltpu.VMEM(parent_state.shape, F32),
            pltpu.VMEM((2, 2, LEVELS, columns), F32),
            pltpu.VMEM((3, rows + 2 * NSTEP, LEVELS, columns), F32),
            pltpu.SemaphoreType.DMA((1 + 2 * (FIELDS + 1) + 2 * rows,)),
        ],
        compiler_params=params(),
        cost_estimate=cost(40_000_000, 8_000_000),
        name="parent_run",
    )(meta, wave_speed, parent_state, near, far, metrics, after)


def reorder_kernel(meta_ref, in_ref, after_ref, out_ref, token_ref, sem):
    count = meta_ref.shape[0] - META
    size = in_ref.shape[0] // count

    def start(index, carry):
        source = in_ref.at[pl.ds(meta_ref[META + index] * size, size)]
        pltpu.make_async_copy(source, out_ref.at[pl.ds(index * size, size)], sem).start()
        return carry

    lax.fori_loop(0, count, start, 0)
    pltpu.make_async_copy(in_ref, out_ref, sem).wait()


def reorder(meta, pieces, after):
    return pl.pallas_call(
        reorder_kernel,
        out_shape=(jax.ShapeDtypeStruct(pieces.shape, F32), TOKEN),
        in_specs=[SMEM, VMEM, HBM],
        out_specs=(HBM, HBM),
        scratch_shapes=[pltpu.SemaphoreType.DMA],
        compiler_params=params(),
        cost_estimate=cost(100_000, 200_000),
        name="reorder",
    )(meta, pieces, after)


def insert_kernel(meta_ref, mean_ref, old_ref, parent_ref, out_ref, rows_ref, window_ref, sems):
    first, window = patch_window(meta_ref, out_ref.shape[3])
    offset = first - window
    lane = iota((LEVELS, LANES), 1)
    for field in range(FIELDS):
        upper, lower = [], []
        for third in range(3):
            at = 3 * (field * 3 + third)
            tail = mean_ref[at + 2]
            upper.append(jnp.concatenate([mean_ref[at], mean_ref[at + 1]], axis=0))
            lower.append(jnp.concatenate([tail, pltpu.roll(tail, LANES // 2, 1)], axis=0))
        for row in range(PBX):
            turned = []
            for third in range(3):
                piece = upper[third] if row < 8 else lower[third]
                shift = GROUPS * (third - row % 8) % LANES
                turned.append(pltpu.roll(piece, shift, 1) if shift else piece)
            rows_ref[field * PBX + row] = jnp.where(
                lane < GROUPS,
                turned[0],
                jnp.where(lane < 2 * GROUPS, turned[1], jnp.where(lane < PBY, turned[2], 0.0)),
            )
    source = iota((LANES, 2 * LANES), 0)
    target = iota((LANES, 2 * LANES), 1)
    order = chooser(
        (target == offset + 3 * lax.rem(source, GROUPS) + source // GROUPS) & (source < PBY)
    )
    found = pick(rows_ref[...].reshape(FIELDS * PBX * LEVELS, LANES), order, 2)
    found = found.reshape(FIELDS, PBX, LEVELS, 2 * LANES)
    wide = iota((LEVELS, 2 * LANES), 1)
    inside = (wide >= offset) & (wide < offset + PBY)
    copies = []
    for field in range(FIELDS):
        for row in range(PBX):
            window_ref[field, row] = jnp.where(inside, found[field, row], old_ref[field, row])
        copies.append(
            pltpu.make_async_copy(
                window_ref.at[field],
                out_ref.at[field, :, :, pl.ds(window, 2 * LANES)],
                sems.at[field],
            )
        )
        copies[-1].start()
    for copy in copies:
        copy.wait()


def insert(meta, means, window, advanced):
    return pl.pallas_call(
        insert_kernel,
        out_shape=jax.ShapeDtypeStruct(advanced.shape, F32),
        in_specs=[SMEM, VMEM, VMEM, HBM],
        out_specs=HBM,
        scratch_shapes=[
            pltpu.VMEM((FIELDS * PBX, LEVELS, LANES), F32),
            pltpu.VMEM((FIELDS, PBX, LEVELS, 2 * LANES), F32),
            pltpu.SemaphoreType.DMA((FIELDS,)),
        ],
        input_output_aliases={3: 0},
        compiler_params=params(),
        cost_estimate=cost(4_000_000, 2_000_000),
        name="insert",
    )(meta, means, window, advanced)


def body(parent_state, nest_state, metrics, wave_speed, nest_patch):
    count = lax.axis_size("tile")
    rows, columns = parent_state.shape[2:]
    per_device = rows // PBX * (columns // PBY)
    near_pairs = [(i, i ^ 1) for i in range(count)]
    far_pairs = [(i, (i - 1 + 2 * (i % 2)) % count) for i in range(count)]
    parent_state = jnp.transpose(parent_state, (0, 2, 1, 3))
    nest_state = jnp.transpose(nest_state, (0, 1, 3, 2, 4))

    meta, slots, near, far = prepare(nest_patch, parent_state, metrics, per_device)
    recv = lax.all_to_all(slots, "tile", 0, 0, tiled=True)
    start = nest_in(nest_state)
    recv, near, far, start = lax.optimization_barrier((recv, near, far, start))
    near = lax.ppermute(near, "tile", near_pairs)
    far = lax.ppermute(far, "tile", far_pairs)
    direct = 15 <= count <= 16
    share = -(-15 * PBX // count)
    final, means, nested = nest_run(meta, wave_speed, recv, start, count if direct else 15)
    if not direct:
        means = means.reshape(15 * PBX, LANES)
        means = jnp.pad(means, ((0, count * share - 15 * PBX), (0, 0)))
        means = means.reshape(count, share, LANES)
    spread = lax.all_to_all(means, "tile", 0, 0, tiled=True)
    nest_next, unpacked = nest_out(final, nested)
    mixed, ordered = reorder(meta, spread, unpacked)
    returned = lax.all_to_all(mixed, "tile", 0, 0, tiled=True)
    advanced, window = parent_run(meta, wave_speed, parent_state, near, far, metrics, ordered)
    if not direct:
        returned = returned.reshape(count * share, LANES)[: 15 * PBX].reshape(45, 4, LANES)
    parent_next = insert(meta, returned, window, advanced)
    return (jnp.transpose(parent_next, (0, 2, 1, 3)), jnp.transpose(nest_next, (0, 1, 3, 2, 4)))


def solution(mesh):
    in_specs = (
        P(None, None, ("member", "tile"), None),
        P(("member", "tile"), None, None, None, None),
        P(None, "tile", None),
        P(),
        P(),
    )
    out_specs = (
        P(None, None, ("member", "tile"), None),
        P(("member", "tile"), None, None, None, None),
    )
    return jax.shard_map(body, mesh=mesh, in_specs=in_specs, out_specs=out_specs, check_vma=False)
```
